32 devices in a mesh: gx: 8 (over z, x), gy: 4 (over y, core).
Axes of the slice: x: 2, y: 2, z: 4, core: 2. Of those that a mesh axis runs over, the one named last changes fastest.
Arguments:
- electric: float32 [3, 256, 64, 128], P(None, 'gx', 'gy'), may hold values from -6 to 6
- magnetic: float32 [3, 256, 64, 128], P(None, 'gx', 'gy'), may hold values from -6 to 6
- material: int32 [256, 64, 128], P('gx', 'gy'), may hold values from 0 to 3
- pml_flags: int32 [256, 64, 128], P('gx', 'gy'), may hold values 0 or 1
- permittivity: float32 [4], replicated, may hold values from 1 to 12
- pml_sigma: float32 [128], replicated, may hold values from 0.05 to 1
- omega: float32 [8], replicated, may hold values from 0.5 to 3
Outputs:
- electric_out: float32 [3, 256, 64, 128], P(None, 'gx', 'gy')
- magnetic_out: float32 [3, 256, 64, 128], P(None, 'gx', 'gy')
- spectra: float32 [16, 2, 256, 64], P('gy', None, 'gx')
The draws below stay inside these ranges and needn't reach their ends.
All inputs are finite; a program needn't handle non-finite values. No bound on the sum of `pml_flags` on one device may be relied on, other than what follows from the above.
Results may differ from the reference program's by a relative error of at most 0.00002.
Values sent between devices are 32-bit elements; how exact they have to be, the bound alone decides.
A program may use at most 64 MiB of HBM per device.

```python
import math
import jax
import jax.numpy as jnp
from jax import lax

STEPS = 2
NFREQ = 8
NMAT = 4
NX = 256
NY = 64
NZ = 128


def set_ends(array, rng, least, largest):
    longest = array.shape.index(max(array.shape))
    spots = []
    for shift in (0, 1):
        where = [jax.random.randint(jax.random.fold_in(rng, axis), (), 0, length) for axis, length in enumerate(array.shape)]
        where[longest] = (where[longest] + shift) % array.shape[longest]
        spots.append(tuple(where))
    return array.at[spots[0]].set(least).at[spots[1]].set(largest)


def shard_levels(own_key, shape, pieces, least, top_value):
    loudness = 1.0
    for axis_at, blocks in pieces:
        heights = jax.random.uniform(jax.random.fold_in(jax.random.fold_in(own_key, 6), axis_at), (blocks,), jnp.float32, least / len(pieces), top_value / len(pieces))
        loudness = loudness * jnp.repeat(jnp.exp(heights), shape[axis_at] // blocks).reshape((-1,) + (1,) * (len(shape) - 1 - axis_at))
    return loudness


def normal_values(key, extent, spread, limit, shards=(), dtype=jnp.bfloat16):
    entries = jax.random.normal(key, extent, jnp.float32) * spread
    if len(shards) > 0:
        entries = shard_levels(key, extent, shards, -0.22, 0.18) * entries
    return jnp.clip(entries, min=-limit, max=limit).astype(dtype)


def setup_inputs(seed: int = 0) -> dict:
    key_of = jax.random.split(jax.random.key(seed), 8)
    return {
        "electric": normal_values(key_of[0], (3, NX, NY, NZ), 1.0, 6.0, ((1, 8), (2, 4)), jnp.float32),
        "magnetic": normal_values(key_of[1], (3, NX, NY, NZ), 1.0, 6.0, ((1, 8), (2, 4)), jnp.float32),
        "material": set_ends(jax.random.randint(key_of[2], (NX, NY, NZ), 0, NMAT), jax.random.fold_in(key_of[2], 1), 0, NMAT - 1).astype(jnp.int32),
        "pml_flags": set_ends((jax.random.randint(key_of[3], (NX, NY, NZ), 0, 3) < 1).astype(jnp.int32), jax.random.fold_in(key_of[3], 1), 0, 1),
        "permittivity": jnp.clip(jnp.exp(jax.random.uniform(key_of[4], (NMAT,), jnp.float32, math.log(1.0), math.log(12.0))), 1.0, 12.0),
        "pml_sigma": jnp.clip(jnp.exp(jax.random.uniform(key_of[5], (NZ,), jnp.float32, math.log(0.05), math.log(1.0))), 0.05, 1.0),
        "omega": jnp.clip(jnp.exp(jax.random.uniform(key_of[6], (NFREQ,), jnp.float32, math.log(0.5), math.log(3.0))), 0.5, 3.0),
    }


time_step = 0.5


def forward_diff(field, axis):
    rest = lax.slice_in_dim(field, 1, field.shape[axis], axis=axis)
    edge = jnp.zeros_like(lax.slice_in_dim(field, 0, 1, axis=axis))
    return jnp.concatenate([rest, edge], axis=axis) - field


def backward_diff(field, axis):
    rest = lax.slice_in_dim(field, 0, field.shape[axis] - 1, axis=axis)
    edge = jnp.zeros_like(lax.slice_in_dim(field, 0, 1, axis=axis))
    return field - jnp.concatenate([edge, rest], axis=axis)


def reference(electric, magnetic, material, pml_flags, permittivity, pml_sigma, omega):
    eps_cell = jnp.zeros(material.shape, jnp.float32)
    for index in range(NMAT):
        eps_cell = eps_cell + (material == index).astype(jnp.float32) * permittivity[index]
    sigma_cell = pml_flags.astype(jnp.float32) * pml_sigma[None, None, :]
    s_mag = sigma_cell * time_step / 2.0
    h_keep = (1.0 - s_mag) / (1.0 + s_mag)
    h_gain = time_step / (1.0 + s_mag)
    s_ele = sigma_cell * time_step / (2.0 * eps_cell)
    e_keep = (1.0 - s_ele) / (1.0 + s_ele)
    e_gain = time_step / (eps_cell * (1.0 + s_ele))
    plane_at = electric.shape[3] // 2
    spectra = jnp.zeros((2 * NFREQ, 2, electric.shape[1], electric.shape[2]), jnp.float32)
    for step in range(STEPS):
        moment = (step + 1) * time_step
        coef = jnp.concatenate([jnp.cos(omega * moment), -jnp.sin(omega * moment)])
        ex, ey, ez = electric[0], electric[1], electric[2]
        curl_x = forward_diff(ez, 1) - forward_diff(ey, 2)
        curl_y = forward_diff(ex, 2) - forward_diff(ez, 0)
        curl_z = forward_diff(ey, 0) - forward_diff(ex, 1)
        magnetic = h_keep[None] * magnetic - h_gain[None] * jnp.stack([curl_x, curl_y, curl_z])
        hx, hy, hz = magnetic[0], magnetic[1], magnetic[2]
        curl_x = backward_diff(hz, 1) - backward_diff(hy, 2)
        curl_y = backward_diff(hx, 2) - backward_diff(hz, 0)
        curl_z = backward_diff(hy, 0) - backward_diff(hx, 1)
        electric = e_keep[None] * electric + e_gain[None] * jnp.stack([curl_x, curl_y, curl_z])
        sample = electric[0:2, :, :, plane_at]
        spectra = spectra + coef[:, None, None, None] * sample[None]
    return electric, magnetic, spectra
```

```python
import functools

import jax
import jax.numpy as jnp
from jax import lax
from jax.experimental import pallas as pl
from jax.experimental.pallas import tpu as pltpu
from jax.sharding import PartitionSpec as P

STEPS = 2
NFREQ = 8
NMAT = 4
DT = 0.5
MESH = pl.DeviceIdType.MESH

TOP = 8


def loop(low, high, unroll, body, carry):
    rounds = (high - low) // unroll

    def several(i, carry):
        for k in range(unroll):
            carry = body(low + i * unroll + k, carry)
        return carry

    carry = lax.fori_loop(0, rounds, several, carry)
    for p in range(low + rounds * unroll, high):
        carry = body(p, carry)
    return carry


def kernel(ngx, ngy, nx, ny, nz,
           e_in, h_in, mat_in, flag_in, perm_in, sigma_in, omega_in,
           e_out, h_out, spectra,
           e0, e1, hf, flag, mat, ek, eg, perm, sigma, omega, samp,
           load_sem, store_sem, send1, recv1, send2, recv2, send3, recv3):
    gx, gy = lax.axis_index("gx"), lax.axis_index("gy")
    left, right = gx > 0, gx < ngx - 1
    down, up = gy > 0, gy < ngy - 1
    own_x = pl.ds(1, nx)
    own_y = pl.ds(TOP, ny)
    behind, ahead = TOP - 1, TOP + ny
    last = nx + 1

    loads = [
        pltpu.make_async_copy(e_in, e0.at[:, own_x, own_y], load_sem.at[0]),
        pltpu.make_async_copy(h_in, hf.at[:, own_x, own_y], load_sem.at[1]),
        pltpu.make_async_copy(flag_in, flag.at[own_x, own_y], load_sem.at[2]),
        pltpu.make_async_copy(mat_in, mat, load_sem.at[3]),
        pltpu.make_async_copy(sigma_in, sigma, load_sem.at[4]),
    ]
    for copy in loads:
        copy.start()

    barrier = pltpu.get_barrier_semaphore()
    partners = [
        (left, (gx - 1, gy)),
        (right, (gx + 1, gy)),
        (left & up, (gx - 1, gy + 1)),
        (right & down, (gx + 1, gy - 1)),
    ]
    expected = ngy - 1
    for there, device in partners:
        expected = expected + there.astype(jnp.int32)

        @pl.when(there)
        def _():
            pl.semaphore_signal(barrier, inc=1, device_id=device, device_id_type=MESH)

    for d in range(1, ngy):
        pl.semaphore_signal(barrier, inc=1, device_id=(gx, lax.rem(gy + d, ngy)), device_id_type=MESH)

    @pl.when(jnp.logical_not(right))
    def _():
        for e in (e0, e1):
            for c in (1, 2):
                e[c, last, 0:ahead] = jnp.zeros((ahead, nz), jnp.float32)

    @pl.when(jnp.logical_not(up))
    def _():
        for e in (e0, e1):
            for c in (0, 2):
                e[c, 0:last, ahead:ahead + 8] = jnp.zeros((last, 8, nz), jnp.float32)

    pl.semaphore_wait(barrier, expected)

    def remote(src, dst, sends, recvs, i, device):
        return pltpu.make_async_remote_copy(
            src_ref=src, dst_ref=dst, send_sem=sends.at[i], recv_sem=recvs.at[i],
            device_id=device, device_id_type=MESH)

    def e_halo(src, x_of, y_of, e, sends, recvs):
        at = functools.partial(remote, sends=sends, recvs=recvs)
        xs = pl.ds(x_of(0), nx)
        ys = pl.ds(y_of(0), ny)
        to_left = [at(src.at[1:3, x_of(0), ys], e.at[1:3, last, own_y], i=0, device=(gx - 1, gy))]
        to_right = [at(src.at[:, x_of(nx - 1), ys], e.at[:, 0, own_y], i=1, device=(gx + 1, gy))]
        to_down = [at(src.at[c, xs, y_of(0)], e.at[c, own_x, ahead], i=2 + c // 2, device=(gx, gy - 1)) for c in (0, 2)]
        to_up = [at(src.at[:, xs, y_of(ny - 1)], e.at[:, own_x, behind], i=4, device=(gx, gy + 1))]
        corner_lu = [at(src.at[1, x_of(0), y_of(ny - 1)], e.at[1, last, behind], i=5, device=(gx - 1, gy + 1))]
        corner_rd = [at(src.at[0, x_of(nx - 1), y_of(0)], e.at[0, 0, ahead], i=6, device=(gx + 1, gy - 1))]
        return [
            [left, right, to_left],
            [right, left, to_right],
            [down, up, to_down],
            [up, down, to_up],
            [left & up, right & down, corner_lu],
            [right & down, left & up, corner_rd],
        ]

    def start(plan):
        for sends, _, copies in plan:
            @pl.when(sends)
            def _():
                for copy in copies:
                    copy.start()

    def wait_recv(plan):
        for _, receives, copies in plan:
            @pl.when(receives)
            def _():
                for copy in copies:
                    copy.wait_recv()

    def wait_send(plan):
        for sends, _, copies in plan:
            @pl.when(sends)
            def _():
                for copy in copies:
                    copy.wait_send()

    round1 = e_halo(e_in, lambda x: x, lambda y: y, e0, send1, recv1)
    at1 = functools.partial(remote, sends=send1, recvs=recv1)
    round1[1][2] += [
        at1(h_in.at[1:3, nx - 1], hf.at[1:3, 0, own_y], i=7, device=(gx + 1, gy)),
        at1(flag_in.at[nx - 1], flag.at[0, own_y], i=8, device=(gx + 1, gy)),
    ]
    round1[3][2] += [
        at1(h_in.at[0, :, ny - 1], hf.at[0, own_x, behind], i=9, device=(gx, gy + 1)),
        at1(h_in.at[2, :, ny - 1], hf.at[2, own_x, behind], i=10, device=(gx, gy + 1)),
        at1(flag_in.at[:, ny - 1], flag.at[own_x, behind], i=11, device=(gx, gy + 1)),
    ]
    start(round1)

    loads[4].wait()
    sg = sigma[...]
    sm = sg * DT / 2.0
    hk1 = (1.0 - sm) / (1.0 + sm)
    hg1 = DT / (1.0 + sm)
    ek1, eg1, eg0 = [], [], []
    for m in range(NMAT):
        eps = jnp.full((1, nz), perm_in[m], jnp.float32)
        se = sg * DT / (2.0 * eps)
        ek1.append((1.0 - se) / (1.0 + se))
        eg1.append(DT / (eps * (1.0 + se)))
        eg0.append(DT / eps)

    def lanes(n):
        return lax.broadcasted_iota(jnp.int32, (n, nz), 1)

    def next_z(f):
        return jnp.where(lanes(f.shape[0]) == nz - 1, 0.0, pltpu.roll(f, nz - 1, 1))

    def prev_z(f):
        return jnp.where(lanes(f.shape[0]) == 0, 0.0, pltpu.roll(f, 1, 1))

    def h_update(e, p, r, n, comps, keep=None):
        at, nxt = slice(r, r + n), slice(r + 1, r + n + 1)
        absorbs = flag[p, at] == 1
        hk = jnp.where(absorbs, hk1, 1.0)
        hg = jnp.where(absorbs, hg1, DT)
        ex, ey, ez = e[0, p, at], e[1, p, at], e[2, p, at]
        for c in comps:
            if c == 0:
                curl = (e[2, p, nxt] - ez) - (next_z(ey) - ey)
            elif c == 1:
                curl = (next_z(ex) - ex) - (e[2, p + 1, at] - ez)
            else:
                curl = (e[1, p + 1, at] - ey) - (e[0, p, nxt] - ex)
            new = hk * hf[c, p, at] - hg * curl
            if keep is not None:
                new = jnp.where(keep, new, 0.0)
            hf[c, p, at] = new

    tiles = ny // 8

    def h_inner(e):
        def body(p, carry):
            h_update(e, p, TOP, ny - 8, (0, 1, 2))
            return carry
        loop(1, nx, 4, body, 0)

    def h_outer(e):
        def body(p, carry):
            h_update(e, p, TOP + ny - 8, 8, (0, 1, 2))
            h_update(e, p, 0, 8, (0, 2), down)
            return carry
        h_update(e, 0, TOP, ny, (1, 2), left)
        h_update(e, nx, TOP, ny - 8, (0, 1, 2))
        loop(1, nx + 1, 4, body, 0)

    at = slice(TOP, TOP + ny)
    below = slice(TOP - 1, TOP + ny - 1)

    def e_update(step, src, dst, p, acc):
        hx, hy, hz = hf[0, p, at], hf[1, p, at], hf[2, p, at]
        keep, gain = ek[p - 1], eg[p - 1]
        curls = (
            lambda: (hz - hf[2, p, below]) - (hy - prev_z(hy)),
            lambda: (hx - prev_z(hx)) - (hz - hf[2, p - 1, at]),
            lambda: (hy - hf[1, p - 1, at]) - (hx - hf[0, p, below]),
        )
        for c in range(3):
            new = keep * src[c, p, at] + gain * curls[c]()
            dst[c, p, at] = new
            if c < 2:
                column = jnp.broadcast_to(new[:, nz // 2:nz // 2 + 1], (ny, nz))
                acc = jnp.where(lanes(ny) == (step * 2 + c) * nx + p - 1, column, acc)
        return acc

    loads[2].wait()
    loads[3].wait()

    def e_coefficients(p, carry):
        m = mat[p]
        absorbs = flag[p + 1, at] == 1
        k, g1, g0 = ek1[NMAT - 1], eg1[NMAT - 1], eg0[NMAT - 1]
        for i in range(NMAT - 2, -1, -1):
            here = m == i
            k = jnp.where(here, ek1[i], k)
            g1 = jnp.where(here, eg1[i], g1)
            g0 = jnp.where(here, eg0[i], g0)
        ek[p] = jnp.where(absorbs, k, 1.0)
        eg[p] = jnp.where(absorbs, g1, g0)
        return carry

    loop(0, nx, 4, e_coefficients, 0)
    loads[0].wait()
    loads[1].wait()
    h_inner(e0)
    wait_recv(round1)
    h_outer(e0)
    acc = jnp.zeros((ny, nz), jnp.float32)
    round2 = e_halo(e1, lambda x: x + 1, lambda y: y + TOP, e1, send2, recv2)
    for p in (1, nx):
        acc = e_update(0, e0, e1, p, acc)
    start(round2[0:2] + round2[4:6])
    acc = loop(2, nx, 4, functools.partial(e_update, 0, e0, e1), acc)
    start(round2[2:4])

    h_inner(e1)
    wait_recv(round2)
    h_outer(e1)
    stores = [
        pltpu.make_async_copy(hf.at[:, own_x, own_y], h_out, store_sem.at[0]),
        pltpu.make_async_copy(e0.at[:, own_x, own_y], e_out, store_sem.at[1]),
    ]
    stores[0].start()
    acc = loop(1, nx + 1, 4, functools.partial(e_update, 1, e1, e0), acc)
    mine = pl.ds(pl.multiple_of(gy * ny, ny), ny)
    samp[mine] = acc
    round3 = []
    for d in range(1, ngy):
        mate = lax.rem(gy + d, ngy)
        copy = pltpu.make_async_remote_copy(
            src_ref=samp.at[mine], dst_ref=samp.at[mine], send_sem=send3.at[d], recv_sem=recv3.at[d],
            device_id=(gx, mate), device_id_type=MESH)
        copy.start()
        round3.append(copy)
    stores[1].start()

    slots = spectra.shape[0]
    rows = lax.broadcasted_iota(jnp.int32, (8, nz), 0)
    angle = jnp.zeros((8, nz), jnp.float32)
    for n in range(STEPS):
        for k in range(slots):
            w = omega_in[lax.rem(gy * slots + k, NFREQ)]
            angle = jnp.where(rows == n * slots + k, w * ((n + 1) * DT), angle)
    cosine, sine = jnp.cos(angle), jnp.sin(angle)

    for copy in round3:
        copy.wait_recv()
    table = samp[...].T
    for k in range(slots):
        is_cos = gy * slots + k < NFREQ
        for c in range(2):
            total = None
            for n in range(STEPS):
                row = n * slots + k
                coef = jnp.where(is_cos, cosine[row:row + 1, 0:1], -sine[row:row + 1, 0:1])
                first = (n * 2 + c) * nx
                term = coef * table[first:first + nx]
                total = term if total is None else total + term
            spectra[k, c] = total

    wait_send(round1)
    wait_send(round2)
    for copy in round3:
        copy.wait_send()
    for copy in stores:
        copy.wait()


def solution(mesh):
    ngx, ngy = mesh.shape["gx"], mesh.shape["gy"]

    def local(electric, magnetic, material, pml_flags, permittivity, pml_sigma, omega):
        _, nx, ny, nz = electric.shape
        slots = 2 * NFREQ // ngy
        anywhere = pl.BlockSpec(memory_space=pl.ANY)
        scalars = pl.BlockSpec(memory_space=pltpu.SMEM)
        f32 = jnp.float32
        return pl.pallas_call(
            functools.partial(kernel, ngx, ngy, nx, ny, nz),
            out_shape=(
                jax.ShapeDtypeStruct(electric.shape, f32),
                jax.ShapeDtypeStruct(magnetic.shape, f32),
                jax.ShapeDtypeStruct((slots, 2, nx, ny * ngy), f32),
            ),
            in_specs=[anywhere] * 4 + [scalars, anywhere, scalars],
            out_specs=(anywhere, anywhere, pl.BlockSpec(memory_space=pltpu.VMEM)),
            scratch_shapes=[
                pltpu.VMEM((3, nx + 2, ny + 16, nz), f32),
                pltpu.VMEM((3, nx + 2, ny + 16, nz), f32),
                pltpu.VMEM((3, nx + 1, ny + 8, nz), f32),
                pltpu.VMEM((nx + 1, ny + 8, nz), jnp.int32),
                pltpu.VMEM((nx, ny, nz), jnp.int32),
                pltpu.VMEM((nx, ny, nz), f32),
                pltpu.VMEM((nx, ny, nz), f32),
                pltpu.SMEM((NMAT,), f32),
                pltpu.VMEM((1, nz), f32),
                pltpu.SMEM((NFREQ,), f32),
                pltpu.VMEM((ngy * ny, nz), f32),
                pltpu.SemaphoreType.DMA((5,)),
                pltpu.SemaphoreType.DMA((2,)),
                pltpu.SemaphoreType.DMA((12,)),
                pltpu.SemaphoreType.DMA((12,)),
                pltpu.SemaphoreType.DMA((7,)),
                pltpu.SemaphoreType.DMA((7,)),
                pltpu.SemaphoreType.DMA((ngy,)),
                pltpu.SemaphoreType.DMA((ngy,)),
            ],
            compiler_params=pltpu.CompilerParams(
                collective_id=0, has_side_effects=True, vmem_limit_bytes=24 * 1024 * 1024),
        )(electric, magnetic, material, pml_flags, permittivity, pml_sigma.reshape(1, nz), omega)

    placed = (
        P(None, "gx", "gy", None),
        P(None, "gx", "gy", None),
        P("gx", "gy", None),
        P("gx", "gy", None),
        P(),
        P(),
        P(),
    )
    return jax.shard_map(
        local,
        mesh=mesh,
        in_specs=placed,
        out_specs=(P(None, "gx", "gy", None), P(None, "gx", "gy", None), P("gy", None, "gx", None)),
        check_vma=False,
    )
```

```python
import functools

import jax
import jax.numpy as jnp
from jax import lax
from jax.experimental import pallas as pl
from jax.experimental.pallas import tpu as pltpu
from jax.sharding import PartitionSpec as P

STEPS = 2
NFREQ = 8
NMAT = 4
DT = 0.5
MESH = pl.DeviceIdType.MESH

TOP = 8


BLOCK = 8


def blocks(low, high, body, carry=0):
    return lax.fori_loop(0, (high - low) // BLOCK, lambda i, c: body(low + i * BLOCK, c), carry)


def kernel(ngx, ngy, nx, ny, nz,
           e_in, h_in, mat_in, flag_in, perm_in, sigma_in, omega_in,
           e_out, h_out, samp, weights,
           e0, e1, h0, h1, h2, flag, mat, ek, eg, perm, sigma, omega,
           load_sem, send1, recv1, send2, recv2, send3, recv3):
    gx, gy = lax.axis_index("gx"), lax.axis_index("gy")
    left, right = gx > 0, gx < ngx - 1
    down, up = gy > 0, gy < ngy - 1
    own_x = pl.ds(1, nx)
    own_y = pl.ds(TOP, ny)
    behind, ahead = TOP - 1, TOP + ny
    last = nx + 1

    loads = [
        pltpu.make_async_copy(e_in, e0.at[:, own_x, own_y], load_sem.at[0]),
        pltpu.make_async_copy(h_in, h0.at[:, own_x, own_y], load_sem.at[1]),
        pltpu.make_async_copy(flag_in, flag.at[own_x, own_y], load_sem.at[2]),
        pltpu.make_async_copy(mat_in, mat, load_sem.at[3]),
        pltpu.make_async_copy(sigma_in, sigma, load_sem.at[4]),
        pltpu.make_async_copy(perm_in, perm, load_sem.at[5]),
        pltpu.make_async_copy(omega_in, omega, load_sem.at[6]),
    ]
    for copy in loads:
        copy.start()

    barrier = pltpu.get_barrier_semaphore()
    partners = [
        (left, (gx - 1, gy)),
        (right, (gx + 1, gy)),
        (left & up, (gx - 1, gy + 1)),
        (right & down, (gx + 1, gy - 1)),
    ]
    expected = ngy - 1
    for there, device in partners:
        expected = expected + there.astype(jnp.int32)

        @pl.when(there)
        def _():
            pl.semaphore_signal(barrier, inc=1, device_id=device, device_id_type=MESH)

    for d in range(1, ngy):
        pl.semaphore_signal(barrier, inc=1, device_id=(gx, lax.rem(gy + d, ngy)), device_id_type=MESH)

    @pl.when(jnp.logical_not(right))
    def _():
        for e in (e0, e1):
            for c in (1, 2):
                e[c, last, 0:ahead] = jnp.zeros((ahead, nz), jnp.float32)

    @pl.when(jnp.logical_not(up))
    def _():
        for e in (e0, e1):
            for c in (0, 2):
                e[c, 0:last, ahead:ahead + 8] = jnp.zeros((last, 8, nz), jnp.float32)

    pl.semaphore_wait(barrier, expected)

    def remote(src, dst, sends, recvs, i, device):
        return pltpu.make_async_remote_copy(
            src_ref=src, dst_ref=dst, send_sem=sends.at[i], recv_sem=recvs.at[i],
            device_id=device, device_id_type=MESH)

    def e_halo(src, x_of, y_of, e, sends, recvs):
        at = functools.partial(remote, sends=sends, recvs=recvs)
        xs = pl.ds(x_of(0), nx)
        ys = pl.ds(y_of(0), ny)
        to_left = [at(src.at[1:3, x_of(0), ys], e.at[1:3, last, own_y], i=0, device=(gx - 1, gy))]
        to_right = [at(src.at[:, x_of(nx - 1), ys], e.at[:, 0, own_y], i=1, device=(gx + 1, gy))]
        to_down = [at(src.at[c, xs, y_of(0)], e.at[c, own_x, ahead], i=2 + c // 2, device=(gx, gy - 1)) for c in (0, 2)]
        to_up = [at(src.at[:, xs, y_of(ny - 1)], e.at[:, own_x, behind], i=4, device=(gx, gy + 1))]
        corner_lu = [at(src.at[1, x_of(0), y_of(ny - 1)], e.at[1, last, behind], i=5, device=(gx - 1, gy + 1))]
        corner_rd = [at(src.at[0, x_of(nx - 1), y_of(0)], e.at[0, 0, ahead], i=6, device=(gx + 1, gy - 1))]
        return [
            [left, right, to_left],
            [right, left, to_right],
            [down, up, to_down],
            [up, down, to_up],
            [left & up, right & down, corner_lu],
            [right & down, left & up, corner_rd],
        ]

    def start(plan):
        for sends, _, copies in plan:
            @pl.when(sends)
            def _():
                for copy in copies:
                    copy.start()

    def wait_recv(plan):
        for _, receives, copies in plan:
            @pl.when(receives)
            def _():
                for copy in copies:
                    copy.wait_recv()

    def wait_send(plan):
        for sends, _, copies in plan:
            @pl.when(sends)
            def _():
                for copy in copies:
                    copy.wait_send()

    round1 = e_halo(e_in, lambda x: x, lambda y: y, e0, send1, recv1)
    at1 = functools.partial(remote, sends=send1, recvs=recv1)
    round1[1][2] += [
        at1(h_in.at[1:3, nx - 1], h0.at[1:3, 0, own_y], i=7, device=(gx + 1, gy)),
        at1(flag_in.at[nx - 1], flag.at[0, own_y], i=8, device=(gx + 1, gy)),
    ]
    round1[3][2] += [
        at1(h_in.at[0, :, ny - 1], h0.at[0, own_x, behind], i=9, device=(gx, gy + 1)),
        at1(h_in.at[2, :, ny - 1], h0.at[2, own_x, behind], i=10, device=(gx, gy + 1)),
        at1(flag_in.at[:, ny - 1], flag.at[own_x, behind], i=11, device=(gx, gy + 1)),
    ]
    start(round1)

    loads[4].wait()
    loads[5].wait()
    sg = sigma[...]
    sm = sg * DT / 2.0
    hk1 = (1.0 - sm) / (1.0 + sm)
    hg1 = DT / (1.0 + sm)
    ek1, eg1, eg0 = [], [], []
    for m in range(NMAT):
        eps = jnp.full((1, nz), perm[m], jnp.float32)
        se = sg * DT / (2.0 * eps)
        ek1.append((1.0 - se) / (1.0 + se))
        eg1.append(DT / (eps * (1.0 + se)))
        eg0.append(DT / eps)

    def lanes(f):
        return lax.broadcasted_iota(jnp.int32, f.shape, f.ndim - 1)

    def next_z(f):
        return jnp.where(lanes(f) == nz - 1, 0.0, pltpu.roll(f, nz - 1, f.ndim - 1))

    def prev_z(f):
        return jnp.where(lanes(f) == 0, 0.0, pltpu.roll(f, 1, f.ndim - 1))

    def h_update(e, src, dst, p, planes, r, n, comps, keep=None):
        at, nxt = slice(r, r + n), slice(r + 1, r + n + 1)
        ps, ahead_x = pl.ds(p, planes), pl.ds(p + 1, planes)
        absorbs = flag[ps, at] == 1
        hk = jnp.where(absorbs, hk1, 1.0)
        hg = jnp.where(absorbs, hg1, DT)
        ex, ey, ez = e[0, ps, at], e[1, ps, at], e[2, ps, at]
        curls = (
            lambda: (e[2, ps, nxt] - ez) - (next_z(ey) - ey),
            lambda: (next_z(ex) - ex) - (e[2, ahead_x, at] - ez),
            lambda: (e[1, ahead_x, at] - ey) - (e[0, ps, nxt] - ex),
        )
        results = []
        for c in comps:
            new = hk * src[c, ps, at] - hg * curls[c]()
            results.append(new if keep is None else jnp.where(keep, new, 0.0))
        for c, new in zip(comps, results):
            dst[c, ps, at] = new

    low, high = TOP, TOP + ny
    inner_end = 1 + (nx - 1) // BLOCK * BLOCK

    def h_inner(e, src, dst):
        def body(p, carry):
            h_update(e, src, dst, p, BLOCK, low, ny - 8, (0, 1, 2))
            return carry
        blocks(1, inner_end, body)

    def h_outer(e, src, dst):
        def body(p, carry):
            h_update(e, src, dst, p, BLOCK, high - 8, 8, (0, 1, 2))
            h_update(e, src, dst, p, BLOCK, 0, 8, (0, 2), down)
            return carry
        h_update(e, src, dst, 0, 1, low, ny, (1, 2), left)
        h_update(e, src, dst, inner_end, nx + 1 - inner_end, low, ny - 8, (0, 1, 2))
        blocks(1, nx + 1, body)

    def e_update(step, src, h, dst, dst_x, dst_y, p, acc):
        for r in range(0, ny, 8):
            at, below = slice(low + r, low + r + 8), slice(low + r - 1, low + r + 7)
            ps, behind_x = pl.ds(p, BLOCK), pl.ds(p - 1, BLOCK)
            hx, hy, hz = h[0, ps, at], h[1, ps, at], h[2, ps, at]
            keep, gain = ek[behind_x, r:r + 8], eg[behind_x, r:r + 8]
            curls = (
                lambda: (hz - h[2, ps, below]) - (hy - prev_z(hy)),
                lambda: (hx - prev_z(hx)) - (hz - h[2, behind_x, at]),
                lambda: (hy - h[1, behind_x, at]) - (hx - h[0, ps, below]),
            )
            news = [keep * src[c, ps, at] + gain * curls[c]() for c in range(3)]
            for c in range(3):
                dst[c, pl.ds(p + dst_x, BLOCK), r + dst_y:r + dst_y + 8] = news[c]
            piece = acc[r // 8]
            for c in range(2):
                for k in range(BLOCK):
                    column = jnp.broadcast_to(news[c][k, :, nz // 2:nz // 2 + 1], (8, nz))
                    piece = jnp.where(lanes(piece) == (step * 2 + c) * nx + p - 1 + k, column, piece)
            acc = acc[:r // 8] + (piece,) + acc[r // 8 + 1:]
        return acc

    loads[2].wait()
    loads[3].wait()

    def e_coefficients(p, carry):
        ps = pl.ds(p, BLOCK)
        m = mat[ps]
        absorbs = flag[pl.ds(p + 1, BLOCK), low:high] == 1
        k, g1, g0 = ek1[NMAT - 1], eg1[NMAT - 1], eg0[NMAT - 1]
        for i in range(NMAT - 2, -1, -1):
            here = m == i
            k = jnp.where(here, ek1[i], k)
            g1 = jnp.where(here, eg1[i], g1)
            g0 = jnp.where(here, eg0[i], g0)
        ek[ps] = jnp.where(absorbs, k, 1.0)
        eg[ps] = jnp.where(absorbs, g1, g0)
        return carry

    blocks(0, nx, e_coefficients)
    loads[0].wait()
    loads[1].wait()
    h_inner(e0, h0, h1)
    wait_recv(round1)
    h_outer(e0, h0, h1)
    acc = tuple(jnp.zeros((8, nz), jnp.float32) for _ in range(ny // 8))
    step1 = functools.partial(e_update, 0, e0, h1, e1, 0, TOP)
    round2 = e_halo(e1, lambda x: x + 1, lambda y: y + TOP, e1, send2, recv2)
    acc = step1(1, acc)
    acc = step1(nx + 1 - BLOCK, acc)
    start(round2[0:2] + round2[4:6])
    acc = blocks(1 + BLOCK, nx + 1 - BLOCK, step1, acc)
    start(round2[2:4])

    h_inner(e1, h1, h2)
    wait_recv(round2)
    h_outer(e1, h1, h2)
    acc = blocks(1, nx + 1, functools.partial(e_update, 1, e1, h2, e_out, -1, 0), acc)
    mine = pl.ds(pl.multiple_of(gy * ny, ny), ny)
    samp[mine] = jnp.concatenate(acc, axis=0)
    round3 = []
    for d in range(1, ngy):
        mate = lax.rem(gy + d, ngy)
        copy = pltpu.make_async_remote_copy(
            src_ref=samp.at[mine], dst_ref=samp.at[mine], send_sem=send3.at[d], recv_sem=recv3.at[d],
            device_id=(gx, mate), device_id_type=MESH)
        copy.start()
        round3.append(copy)
    h_out[...] = h2[:, 1:nx + 1, low:high]
    loads[6].wait()
    slots = 2 * NFREQ // ngy
    rows = lax.broadcasted_iota(jnp.int32, (8, nz), 0)
    angle = jnp.zeros((8, nz), jnp.float32)
    is_cos = jnp.zeros((8, nz), jnp.bool_)
    for n in range(STEPS):
        for k in range(slots):
            here = rows == n * slots + k
            slot = gy * slots + k
            angle = jnp.where(here, omega[lax.rem(slot, NFREQ)] * ((n + 1) * DT), angle)
            is_cos = is_cos | (here & (slot < NFREQ))
    weights[...] = jnp.where(is_cos, jnp.cos(angle), -jnp.sin(angle))
    wait_send(round1)
    wait_send(round2)
    for copy in round3:
        copy.wait_recv()
    for copy in round3:
        copy.wait_send()


def finish(nx, e_in, h_in, samp, weights, e_out, h_out, spectra_out, spectra, sems):
    copies = [
        pltpu.make_async_copy(e_in, e_out, sems.at[0]),
        pltpu.make_async_copy(h_in, h_out, sems.at[1]),
        pltpu.make_async_copy(spectra, spectra_out, sems.at[2]),
    ]
    copies[0].start()
    copies[1].start()
    slots = spectra.shape[0]
    table = samp[...].T
    for k in range(slots):
        for c in range(2):
            total = None
            for n in range(STEPS):
                row = n * slots + k
                coef = weights[row:row + 1, 0:1]
                first = (n * 2 + c) * nx
                term = coef * table[first:first + nx]
                total = term if total is None else total + term
            spectra[k, c] = total
    copies[2].start()
    for copy in copies:
        copy.wait()


def solution(mesh):
    ngx, ngy = mesh.shape["gx"], mesh.shape["gy"]

    def local(electric, magnetic, material, pml_flags, permittivity, pml_sigma, omega):
        _, nx, ny, nz = electric.shape
        slots = 2 * NFREQ // ngy
        hbm = pl.BlockSpec(memory_space=pltpu.HBM)
        vmem = pl.BlockSpec(memory_space=pltpu.VMEM)
        f32 = jnp.float32
        field = jax.ShapeDtypeStruct(electric.shape, f32)
        e_scratch = pltpu.VMEM((3, nx + 2, ny + 16, nz), f32)
        h_scratch = pltpu.VMEM((3, nx + 1, ny + 8, nz), f32)
        operands = (electric, magnetic, material, pml_flags, permittivity, pml_sigma.reshape(1, nz), omega)
        e_done, h_done, samples, weights = pl.pallas_call(
            functools.partial(kernel, ngx, ngy, nx, ny, nz),
            out_shape=(
                pltpu.VMEM(field.shape, f32),
                pltpu.VMEM(field.shape, f32),
                pltpu.VMEM((ngy * ny, nz), f32),
                pltpu.VMEM((8, nz), f32),
            ),
            in_specs=[hbm] * 7,
            out_specs=(vmem, vmem, vmem, vmem),
            scratch_shapes=[
                e_scratch,
                e_scratch,
                h_scratch,
                h_scratch,
                h_scratch,
                pltpu.VMEM((nx + 1, ny + 8, nz), jnp.int32),
                pltpu.VMEM((nx, ny, nz), jnp.int32),
                pltpu.VMEM((nx, ny, nz), f32),
                pltpu.VMEM((nx, ny, nz), f32),
                pltpu.SMEM((NMAT,), f32),
                pltpu.VMEM((1, nz), f32),
                pltpu.SMEM((NFREQ,), f32),
                pltpu.SemaphoreType.DMA((7,)),
                pltpu.SemaphoreType.DMA((12,)),
                pltpu.SemaphoreType.DMA((12,)),
                pltpu.SemaphoreType.DMA((7,)),
                pltpu.SemaphoreType.DMA((7,)),
                pltpu.SemaphoreType.DMA((ngy,)),
                pltpu.SemaphoreType.DMA((ngy,)),
            ],
            compiler_params=pltpu.CompilerParams(
                collective_id=0, has_side_effects=True, vmem_limit_bytes=24 * 1024 * 1024),
        )(*[pltpu.with_memory_space_constraint(a, pltpu.HBM) for a in operands])
        spectra = jax.ShapeDtypeStruct((slots, 2, nx, ny * ngy), f32)
        return pl.pallas_call(
            functools.partial(finish, nx),
            out_shape=(field, field, spectra),
            in_specs=[vmem] * 4,
            out_specs=(hbm, hbm, hbm),
            scratch_shapes=[pltpu.VMEM(spectra.shape, f32), pltpu.SemaphoreType.DMA((3,))],
            compiler_params=pltpu.CompilerParams(vmem_limit_bytes=24 * 1024 * 1024),
        )(e_done, h_done, samples, weights)

    placed = (
        P(None, "gx", "gy", None),
        P(None, "gx", "gy", None),
        P("gx", "gy", None),
        P("gx", "gy", None),
        P(),
        P(),
        P(),
    )
    return jax.shard_map(
        local,
        mesh=mesh,
        in_specs=placed,
        out_specs=(P(None, "gx", "gy", None), P(None, "gx", "gy", None), P("gy", None, "gx", None)),
        check_vma=False,
    )
```

```python
import functools

import jax
import jax.numpy as jnp
from jax import lax
from jax.experimental import pallas as pl
from jax.experimental.pallas import tpu as pltpu
from jax.sharding import PartitionSpec as P

STEPS = 2
NFREQ = 8
NMAT = 4
DT = 0.5
MESH = pl.DeviceIdType.MESH

TOP = 8


BLOCK = 8


def blocks(low, high, body, carry=0):
    for p in range(low, high, BLOCK):
        carry = body(p, carry)
    return carry


def kernel(ngx, ngy, nx, ny, nz,
           e_in, h_in, mat_in, flag_in, perm_in, sigma_in, omega_in,
           e_out, h_out, samp, weights,
           e0, e1, h0, h1, h2, flag, mat, ek, eg, perm, sigma, omega,
           load_sem, send1, recv1, send2, recv2, send3, recv3):
    gx, gy = lax.axis_index("gx"), lax.axis_index("gy")
    left, right = gx > 0, gx < ngx - 1
    down, up = gy > 0, gy < ngy - 1
    own_x = pl.ds(1, nx)
    own_y = pl.ds(TOP, ny)
    behind, ahead = TOP - 1, TOP + ny
    last = nx + 1

    loads = [
        pltpu.make_async_copy(e_in, e0.at[:, own_x, own_y], load_sem.at[0]),
        pltpu.make_async_copy(h_in, h0.at[:, own_x, own_y], load_sem.at[1]),
        pltpu.make_async_copy(flag_in, flag.at[own_x, own_y], load_sem.at[2]),
        pltpu.make_async_copy(mat_in, mat, load_sem.at[3]),
        pltpu.make_async_copy(sigma_in, sigma, load_sem.at[4]),
        pltpu.make_async_copy(perm_in, perm, load_sem.at[5]),
        pltpu.make_async_copy(omega_in, omega, load_sem.at[6]),
    ]
    for copy in loads:
        copy.start()

    barrier = pltpu.get_barrier_semaphore()
    partners = [
        (left, (gx - 1, gy)),
        (right, (gx + 1, gy)),
        (left & up, (gx - 1, gy + 1)),
        (right & down, (gx + 1, gy - 1)),
    ]
    expected = ngy - 1
    for there, device in partners:
        expected = expected + there.astype(jnp.int32)

        @pl.when(there)
        def _():
            pl.semaphore_signal(barrier, inc=1, device_id=device, device_id_type=MESH)

    for d in range(1, ngy):
        pl.semaphore_signal(barrier, inc=1, device_id=(gx, lax.rem(gy + d, ngy)), device_id_type=MESH)

    @pl.when(jnp.logical_not(right))
    def _():
        for e in (e0, e1):
            for c in (1, 2):
                e[c, last, 0:ahead] = jnp.zeros((ahead, nz), jnp.float32)

    @pl.when(jnp.logical_not(up))
    def _():
        for e in (e0, e1):
            for c in (0, 2):
                e[c, 0:last, ahead:ahead + 8] = jnp.zeros((last, 8, nz), jnp.float32)

    pl.semaphore_wait(barrier, expected)

    def remote(src, dst, sends, recvs, i, device):
        return pltpu.make_async_remote_copy(
            src_ref=src, dst_ref=dst, send_sem=sends.at[i], recv_sem=recvs.at[i],
            device_id=device, device_id_type=MESH)

    def e_halo(src, x_of, y_of, e, sends, recvs):
        at = functools.partial(remote, sends=sends, recvs=recvs)
        xs = pl.ds(x_of(0), nx)
        ys = pl.ds(y_of(0), ny)
        to_left = [at(src.at[1:3, x_of(0), ys], e.at[1:3, last, own_y], i=0, device=(gx - 1, gy))]
        to_right = [at(src.at[:, x_of(nx - 1), ys], e.at[:, 0, own_y], i=1, device=(gx + 1, gy))]
        to_down = [at(src.at[c, xs, y_of(0)], e.at[c, own_x, ahead], i=2 + c // 2, device=(gx, gy - 1)) for c in (0, 2)]
        to_up = [at(src.at[:, xs, y_of(ny - 1)], e.at[:, own_x, behind], i=4, device=(gx, gy + 1))]
        corner_lu = [at(src.at[1, x_of(0), y_of(ny - 1)], e.at[1, last, behind], i=5, device=(gx - 1, gy + 1))]
        corner_rd = [at(src.at[0, x_of(nx - 1), y_of(0)], e.at[0, 0, ahead], i=6, device=(gx + 1, gy - 1))]
        return [
            [left, right, to_left],
            [right, left, to_right],
            [down, up, to_down],
            [up, down, to_up],
            [left & up, right & down, corner_lu],
            [right & down, left & up, corner_rd],
        ]

    def start(plan):
        for sends, _, copies in plan:
            @pl.when(sends)
            def _():
                for copy in copies:
                    copy.start()

    def wait_recv(plan):
        for _, receives, copies in plan:
            @pl.when(receives)
            def _():
                for copy in copies:
                    copy.wait_recv()

    def wait_send(plan):
        for sends, _, copies in plan:
            @pl.when(sends)
            def _():
                for copy in copies:
                    copy.wait_send()

    round1 = e_halo(e_in, lambda x: x, lambda y: y, e0, send1, recv1)
    at1 = functools.partial(remote, sends=send1, recvs=recv1)
    round1[1][2] += [
        at1(h_in.at[1:3, nx - 1], h0.at[1:3, 0, own_y], i=7, device=(gx + 1, gy)),
        at1(flag_in.at[nx - 1], flag.at[0, own_y], i=8, device=(gx + 1, gy)),
    ]
    round1[3][2] += [
        at1(h_in.at[0, :, ny - 1], h0.at[0, own_x, behind], i=9, device=(gx, gy + 1)),
        at1(h_in.at[2, :, ny - 1], h0.at[2, own_x, behind], i=10, device=(gx, gy + 1)),
        at1(flag_in.at[:, ny - 1], flag.at[own_x, behind], i=11, device=(gx, gy + 1)),
    ]
    start(round1)

    loads[4].wait()
    loads[5].wait()
    sg = sigma[...]
    sm = sg * DT / 2.0
    hk1 = (1.0 - sm) / (1.0 + sm)
    hg1 = DT / (1.0 + sm)
    ek1, eg1, eg0 = [], [], []
    for m in range(NMAT):
        eps = jnp.full((1, nz), perm[m], jnp.float32)
        se = sg * DT / (2.0 * eps)
        ek1.append((1.0 - se) / (1.0 + se))
        eg1.append(DT / (eps * (1.0 + se)))
        eg0.append(DT / eps)

    def lanes(f):
        return lax.broadcasted_iota(jnp.int32, f.shape, f.ndim - 1)

    def next_z(f):
        return jnp.where(lanes(f) == nz - 1, 0.0, pltpu.roll(f, nz - 1, f.ndim - 1))

    def prev_z(f):
        return jnp.where(lanes(f) == 0, 0.0, pltpu.roll(f, 1, f.ndim - 1))

    def h_update(e, src, dst, p, planes, r, n, comps, keep=None):
        at, nxt = slice(r, r + n), slice(r + 1, r + n + 1)
        ps, ahead_x = pl.ds(p, planes), pl.ds(p + 1, planes)
        absorbs = flag[ps, at] == 1
        hk = jnp.where(absorbs, hk1, 1.0)
        hg = jnp.where(absorbs, hg1, DT)
        ex, ey, ez = e[0, ps, at], e[1, ps, at], e[2, ps, at]
        curls = (
            lambda: (e[2, ps, nxt] - ez) - (next_z(ey) - ey),
            lambda: (next_z(ex) - ex) - (e[2, ahead_x, at] - ez),
            lambda: (e[1, ahead_x, at] - ey) - (e[0, ps, nxt] - ex),
        )
        results = []
        for c in comps:
            new = hk * src[c, ps, at] - hg * curls[c]()
            results.append(new if keep is None else jnp.where(keep, new, 0.0))
        for c, new in zip(comps, results):
            dst[c, ps, at] = new

    low, high = TOP, TOP + ny
    inner_end = 1 + (nx - 1) // BLOCK * BLOCK

    def h_inner(e, src, dst):
        def body(p, carry):
            h_update(e, src, dst, p, BLOCK, low, ny - 8, (0, 1, 2))
            return carry
        blocks(1, inner_end, body)

    def h_outer(e, src, dst):
        def body(p, carry):
            h_update(e, src, dst, p, BLOCK, high - 8, 8, (0, 1, 2))
            h_update(e, src, dst, p, BLOCK, 0, 8, (0, 2), down)
            return carry
        h_update(e, src, dst, 0, 1, low, ny, (1, 2), left)
        h_update(e, src, dst, inner_end, nx + 1 - inner_end, low, ny - 8, (0, 1, 2))
        blocks(1, nx + 1, body)

    def e_update(step, src, h, dst, dst_x, dst_y, comps, p, acc):
        for r in range(0, ny, 8):
            at, below = slice(low + r, low + r + 8), slice(low + r - 1, low + r + 7)
            ps, behind_x = pl.ds(p, BLOCK), pl.ds(p - 1, BLOCK)
            hx, hy, hz = h[0, ps, at], h[1, ps, at], h[2, ps, at]
            keep, gain = ek[behind_x, r:r + 8], eg[behind_x, r:r + 8]
            curls = (
                lambda: (hz - h[2, ps, below]) - (hy - prev_z(hy)),
                lambda: (hx - prev_z(hx)) - (hz - h[2, behind_x, at]),
                lambda: (hy - h[1, behind_x, at]) - (hx - h[0, ps, below]),
            )
            news = {c: keep * src[c, ps, at] + gain * curls[c]() for c in comps}
            for c in comps:
                dst[c, pl.ds(p + dst_x, BLOCK), r + dst_y:r + dst_y + 8] = news[c]
            piece = acc[r // 8]
            for c in (c for c in comps if c < 2):
                for k in range(BLOCK):
                    column = jnp.broadcast_to(news[c][k, :, nz // 2:nz // 2 + 1], (8, nz))
                    piece = jnp.where(lanes(piece) == (step * 2 + c) * nx + p - 1 + k, column, piece)
            acc = acc[:r // 8] + (piece,) + acc[r // 8 + 1:]
        return acc

    loads[2].wait()
    loads[3].wait()

    def e_coefficients(p, carry):
        ps = pl.ds(p, BLOCK)
        m = mat[ps]
        absorbs = flag[pl.ds(p + 1, BLOCK), low:high] == 1
        k, g1, g0 = ek1[NMAT - 1], eg1[NMAT - 1], eg0[NMAT - 1]
        for i in range(NMAT - 2, -1, -1):
            here = m == i
            k = jnp.where(here, ek1[i], k)
            g1 = jnp.where(here, eg1[i], g1)
            g0 = jnp.where(here, eg0[i], g0)
        ek[ps] = jnp.where(absorbs, k, 1.0)
        eg[ps] = jnp.where(absorbs, g1, g0)
        return carry

    blocks(0, nx, e_coefficients)
    loads[0].wait()
    loads[1].wait()
    h_inner(e0, h0, h1)
    wait_recv(round1)
    h_outer(e0, h0, h1)
    acc = tuple(jnp.zeros((8, nz), jnp.float32) for _ in range(ny // 8))
    step1 = functools.partial(e_update, 0, e0, h1, e1, 0, TOP, (0, 1, 2))
    round2 = e_halo(e1, lambda x: x + 1, lambda y: y + TOP, e1, send2, recv2)
    acc = step1(1, acc)
    acc = step1(nx + 1 - BLOCK, acc)
    start(round2[0:2] + round2[4:6])
    acc = blocks(1 + BLOCK, nx + 1 - BLOCK, step1, acc)
    start(round2[2:4])

    h_inner(e1, h1, h2)
    wait_recv(round2)
    h_outer(e1, h1, h2)
    step2 = functools.partial(e_update, 1, e1, h2, e_out, -1, 0)
    acc = blocks(1, nx + 1, functools.partial(step2, (0, 1)), acc)
    mine = pl.ds(pl.multiple_of(gy * ny, ny), ny)
    samp[mine] = jnp.concatenate(acc, axis=0)
    round3 = []
    for d in range(1, ngy):
        mate = lax.rem(gy + d, ngy)
        copy = pltpu.make_async_remote_copy(
            src_ref=samp.at[mine], dst_ref=samp.at[mine], send_sem=send3.at[d], recv_sem=recv3.at[d],
            device_id=(gx, mate), device_id_type=MESH)
        copy.start()
        round3.append(copy)
    blocks(1, nx + 1, functools.partial(step2, (2,)), acc)
    h_out[...] = h2[:, 1:nx + 1, low:high]
    loads[6].wait()
    slots = 2 * NFREQ // ngy
    rows = lax.broadcasted_iota(jnp.int32, (8, nz), 0)
    angle = jnp.zeros((8, nz), jnp.float32)
    is_cos = jnp.zeros((8, nz), jnp.bool_)
    for n in range(STEPS):
        for k in range(slots):
            here = rows == n * slots + k
            slot = gy * slots + k
            angle = jnp.where(here, omega[lax.rem(slot, NFREQ)] * ((n + 1) * DT), angle)
            is_cos = is_cos | (here & (slot < NFREQ))
    weights[...] = jnp.where(is_cos, jnp.cos(angle), -jnp.sin(angle))
    wait_send(round1)
    wait_send(round2)
    for copy in round3:
        copy.wait_recv()
    for copy in round3:
        copy.wait_send()


def finish(nx, e_in, h_in, samp, weights, e_out, h_out, spectra_out, spectra, sems):
    copies = [
        pltpu.make_async_copy(e_in, e_out, sems.at[0]),
        pltpu.make_async_copy(h_in, h_out, sems.at[1]),
        pltpu.make_async_copy(spectra, spectra_out, sems.at[2]),
    ]
    copies[0].start()
    copies[1].start()
    slots = spectra.shape[0]
    table = samp[...].T
    for k in range(slots):
        for c in range(2):
            total = None
            for n in range(STEPS):
                row = n * slots + k
                coef = weights[row:row + 1, 0:1]
                first = (n * 2 + c) * nx
                term = coef * table[first:first + nx]
                total = term if total is None else total + term
            spectra[k, c] = total
    copies[2].start()
    for copy in copies:
        copy.wait()


def solution(mesh):
    ngx, ngy = mesh.shape["gx"], mesh.shape["gy"]

    def local(electric, magnetic, material, pml_flags, permittivity, pml_sigma, omega):
        _, nx, ny, nz = electric.shape
        slots = 2 * NFREQ // ngy
        hbm = pl.BlockSpec(memory_space=pltpu.HBM)
        vmem = pl.BlockSpec(memory_space=pltpu.VMEM)
        f32 = jnp.float32
        field = jax.ShapeDtypeStruct(electric.shape, f32)
        e_scratch = pltpu.VMEM((3, nx + 2, ny + 16, nz), f32)
        h_scratch = pltpu.VMEM((3, nx + 1, ny + 8, nz), f32)
        operands = (electric, magnetic, material, pml_flags, permittivity, pml_sigma.reshape(1, nz), omega)
        e_done, h_done, samples, weights = pl.pallas_call(
            functools.partial(kernel, ngx, ngy, nx, ny, nz),
            out_shape=(
                pltpu.VMEM(field.shape, f32),
                pltpu.VMEM(field.shape, f32),
                pltpu.VMEM((ngy * ny, nz), f32),
                pltpu.VMEM((8, nz), f32),
            ),
            in_specs=[hbm] * 7,
            out_specs=(vmem, vmem, vmem, vmem),
            scratch_shapes=[
                e_scratch,
                e_scratch,
                h_scratch,
                h_scratch,
                h_scratch,
                pltpu.VMEM((nx + 1, ny + 8, nz), jnp.int32),
                pltpu.VMEM((nx, ny, nz), jnp.int32),
                pltpu.VMEM((nx, ny, nz), f32),
                pltpu.VMEM((nx, ny, nz), f32),
                pltpu.SMEM((NMAT,), f32),
                pltpu.VMEM((1, nz), f32),
                pltpu.SMEM((NFREQ,), f32),
                pltpu.SemaphoreType.DMA((7,)),
                pltpu.SemaphoreType.DMA((12,)),
                pltpu.SemaphoreType.DMA((12,)),
                pltpu.SemaphoreType.DMA((7,)),
                pltpu.SemaphoreType.DMA((7,)),
                pltpu.SemaphoreType.DMA((ngy,)),
                pltpu.SemaphoreType.DMA((ngy,)),
            ],
            compiler_params=pltpu.CompilerParams(
                collective_id=0, has_side_effects=True, vmem_limit_bytes=24 * 1024 * 1024),
        )(*[pltpu.with_memory_space_constraint(a, pltpu.HBM) for a in operands])
        spectra = jax.ShapeDtypeStruct((slots, 2, nx, ny * ngy), f32)
        return pl.pallas_call(
            functools.partial(finish, nx),
            out_shape=(field, field, spectra),
            in_specs=[vmem] * 4,
            out_specs=(hbm, hbm, hbm),
            scratch_shapes=[pltpu.VMEM(spectra.shape, f32), pltpu.SemaphoreType.DMA((3,))],
            compiler_params=pltpu.CompilerParams(vmem_limit_bytes=24 * 1024 * 1024),
        )(e_done, h_done, samples, weights)

    placed = (
        P(None, "gx", "gy", None),
        P(None, "gx", "gy", None),
        P("gx", "gy", None),
        P("gx", "gy", None),
        P(),
        P(),
        P(),
    )
    return jax.shard_map(
        local,
        mesh=mesh,
        in_specs=placed,
        out_specs=(P(None, "gx", "gy", None), P(None, "gx", "gy", None), P("gy", None, "gx", None)),
        check_vma=False,
    )
```

```python
import functools

import jax
import jax.numpy as jnp
from jax import lax
from jax.experimental import pallas as pl
from jax.experimental.pallas import tpu as pltpu
from jax.sharding import PartitionSpec as P

STEPS = 2
NFREQ = 8
NMAT = 4
DT = 0.5
MESH = pl.DeviceIdType.MESH

TOP = 8


BLOCK = 4


def blocks(low, high, body, carry=0):
    for p in range(low, high, BLOCK):
        carry = body(p, carry)
    return carry


def kernel(ngx, ngy, nx, ny, nz,
           e_in, h_in, mat_in, flag_in, perm_in, sigma_in, omega_in,
           e_out, h_out, samp, weights,
           e0, e1, h0, h1, h2, down0, down1, up0, up1, above0, above1, below0, below1, rim_h, rim_flag_out, rim_flag, flag, mat, ek, eg, perm, sigma, omega,
           load_sem, send1, recv1, send2, recv2, send3, recv3):
    gx, gy = lax.axis_index("gx"), lax.axis_index("gy")
    left, right = gx > 0, gx < ngx - 1
    down, up = gy > 0, gy < ngy - 1
    own_x = pl.ds(1, nx)
    own_y = pl.ds(TOP, ny)
    behind, ahead = TOP - 1, TOP + ny
    last = nx + 1

    loads = [
        pltpu.make_async_copy(e_in, e0.at[:, own_x, own_y], load_sem.at[0]),
        pltpu.make_async_copy(h_in, h0.at[:, own_x, own_y], load_sem.at[1]),
        pltpu.make_async_copy(flag_in, flag.at[own_x, own_y], load_sem.at[2]),
        pltpu.make_async_copy(mat_in, mat, load_sem.at[3]),
        pltpu.make_async_copy(sigma_in, sigma, load_sem.at[4]),
        pltpu.make_async_copy(perm_in, perm, load_sem.at[5]),
        pltpu.make_async_copy(omega_in, omega, load_sem.at[6]),
    ]
    for copy in loads:
        copy.start()

    barrier = pltpu.get_barrier_semaphore()
    partners = [
        (left, (gx - 1, gy)),
        (right, (gx + 1, gy)),
        (left & up, (gx - 1, gy + 1)),
        (right & down, (gx + 1, gy - 1)),
    ]
    expected = ngy - 1
    for there, device in partners:
        expected = expected + there.astype(jnp.int32)

        @pl.when(there)
        def _():
            pl.semaphore_signal(barrier, inc=1, device_id=device, device_id_type=MESH)

    for d in range(1, ngy):
        pl.semaphore_signal(barrier, inc=1, device_id=(gx, lax.rem(gy + d, ngy)), device_id_type=MESH)

    @pl.when(jnp.logical_not(right))
    def _():
        for e in (e0, e1):
            for c in (1, 2):
                e[c, last, 0:ahead] = jnp.zeros((ahead, nz), jnp.float32)

    @pl.when(jnp.logical_not(up))
    def _():
        for e, above in ((e0, above0), (e1, above1)):
            e[0, 0, ahead:ahead + 8] = jnp.zeros((8, nz), jnp.float32)
            above[...] = jnp.zeros((2, nx, nz), jnp.float32)

    for e in (e0, e1):
        for c in (0, 2):
            e[c, 1:last, ahead:ahead + 8] = jnp.zeros((nx, 8, nz), jnp.float32)

    def row_of(ref, c, first, r):
        planes, rows = ref.shape[-3], ref.shape[-2]
        return pl.ds((c * planes + first) * rows + r, nx, stride=rows)

    def get_rows(ref, c, first, r):
        return ref.reshape(-1, nz)[row_of(ref, c, first, r), :]

    def put_rows(ref, c, first, r, value):
        ref.reshape(-1, nz)[row_of(ref, c, first, r), :] = value

    def pack_down(e, down_rows):
        for i, c in enumerate((0, 2)):
            down_rows[i] = get_rows(e, c, 1, TOP)

    def pack_up(e, up_rows):
        for c in range(3):
            up_rows[c] = get_rows(e, c, 1, TOP + ny - 1)

    for i in (0, 1, 2):
        loads[i].wait()
    pack_down(e0, down0)
    pack_up(e0, up0)
    for i, c in enumerate((0, 2)):
        up0[3 + i] = get_rows(h0, c, 1, TOP + ny - 1)
    rim_flag_out[...] = get_rows(flag, 0, 1, TOP + ny - 1)

    pl.semaphore_wait(barrier, expected)

    def remote(src, dst, sends, recvs, i, device):
        return pltpu.make_async_remote_copy(
            src_ref=src, dst_ref=dst, send_sem=sends.at[i], recv_sem=recvs.at[i],
            device_id=device, device_id_type=MESH)

    def e_halo(e, down_rows, up_rows, above, below, sends, recvs):
        at = functools.partial(remote, sends=sends, recvs=recvs)
        rim_up = TOP + ny - 1
        to_left = [at(e.at[1:3, 1, own_y], e.at[1:3, last, own_y], i=0, device=(gx - 1, gy))]
        to_right = [at(e.at[:, nx, own_y], e.at[:, 0, own_y], i=1, device=(gx + 1, gy))]
        to_down = [at(down_rows, above, i=2, device=(gx, gy - 1))]
        to_up = [at(up_rows, below.at[:, 0:nx], i=3, device=(gx, gy + 1))]
        corner_lu = [at(e.at[1, 1, rim_up], e.at[1, last, behind], i=4, device=(gx - 1, gy + 1))]
        corner_rd = [at(e.at[0, nx, TOP], e.at[0, 0, ahead], i=5, device=(gx + 1, gy - 1))]
        return [
            [left, right, to_left],
            [right, left, to_right],
            [down, up, to_down],
            [up, down, to_up],
            [left & up, right & down, corner_lu],
            [right & down, left & up, corner_rd],
        ]

    def start(plan):
        for sends, _, copies in plan:
            @pl.when(sends)
            def _():
                for copy in copies:
                    copy.start()

    def wait_recv(plan):
        for _, receives, copies in plan:
            @pl.when(receives)
            def _():
                for copy in copies:
                    copy.wait_recv()

    def wait_send(plan):
        for sends, _, copies in plan:
            @pl.when(sends)
            def _():
                for copy in copies:
                    copy.wait_send()

    round1 = e_halo(e0, down0, up0, above0, below0, send1, recv1)
    at1 = functools.partial(remote, sends=send1, recvs=recv1)
    round1[1][2] += [
        at1(h0.at[1:3, nx, own_y], h0.at[1:3, 0, own_y], i=6, device=(gx + 1, gy)),
        at1(flag.at[nx, own_y], flag.at[0, own_y], i=7, device=(gx + 1, gy)),
    ]
    round1[3][2] += [at1(rim_flag_out, rim_flag, i=8, device=(gx, gy + 1))]
    start(round1)

    loads[4].wait()
    loads[5].wait()
    sg = sigma[...]
    sm = sg * DT / 2.0
    hk1 = (1.0 - sm) / (1.0 + sm)
    hg1 = DT / (1.0 + sm)
    ek1, eg1, eg0 = [], [], []
    for m in range(NMAT):
        eps = jnp.full((1, nz), perm[m], jnp.float32)
        se = sg * DT / (2.0 * eps)
        ek1.append((1.0 - se) / (1.0 + se))
        eg1.append(DT / (eps * (1.0 + se)))
        eg0.append(DT / eps)

    def lanes(f):
        return lax.broadcasted_iota(jnp.int32, f.shape, f.ndim - 1)

    def next_z(f):
        return jnp.where(lanes(f) == nz - 1, 0.0, pltpu.roll(f, nz - 1, f.ndim - 1))

    def prev_z(f):
        return jnp.where(lanes(f) == 0, 0.0, pltpu.roll(f, 1, f.ndim - 1))

    def h_update(e, src, dst, p, planes, r, n, comps, keep=None):
        at, nxt = slice(r, r + n), slice(r + 1, r + n + 1)
        ps, ahead_x = pl.ds(p, planes), pl.ds(p + 1, planes)
        absorbs = flag[ps, at] == 1
        hk = jnp.where(absorbs, hk1, 1.0)
        hg = jnp.where(absorbs, hg1, DT)
        ex, ey, ez = e[0, ps, at], e[1, ps, at], e[2, ps, at]
        curls = (
            lambda: (e[2, ps, nxt] - ez) - (next_z(ey) - ey),
            lambda: (next_z(ex) - ex) - (e[2, ahead_x, at] - ez),
            lambda: (e[1, ahead_x, at] - ey) - (e[0, ps, nxt] - ex),
        )
        for c in comps:
            new = hk * src[c, ps, at] - hg * curls[c]()
            dst[c, ps, at] = new if keep is None else jnp.where(keep, new, 0.0)

    low, high = TOP, TOP + ny
    inner_end = 1 + (nx - 1) // BLOCK * BLOCK

    def h_inner(e, src, dst):
        def body(p, carry):
            h_update(e, src, dst, p, BLOCK, low, ny, (0, 1, 2))
            return carry
        blocks(1, inner_end, body)

    def h_rows(ex, ey, ez, ey_x, ex_y, ez_y, absorbs, hx, hz):
        hk = jnp.where(absorbs, hk1, 1.0)
        hg = jnp.where(absorbs, hg1, DT)
        return (hk * hx - hg * ((ez_y - ez) - (next_z(ey) - ey)),
                hk * hz - hg * ((ey_x - ey) - (ex_y - ex)))

    def h_outer(e, src, dst, down_rows, up_rows, above, below, rim):
        h_update(e, src, dst, 0, 1, low, ny, (1, 2), left)
        h_update(e, src, dst, inner_end, nx + 1 - inner_end, low, ny, (0, 1, 2))
        r = high - 1
        hx, hz = h_rows(
            up_rows[0], up_rows[1], up_rows[2], get_rows(e, 1, 2, r), above[0], above[1],
            get_rows(flag, 0, 1, r) == 1, get_rows(src, 0, 1, r), get_rows(src, 2, 1, r))
        put_rows(dst, 0, 1, r, hx)
        put_rows(dst, 2, 1, r, hz)
        below[1, nx:nx + 1] = e[1, last, behind:behind + 1]
        hx, hz = h_rows(
            below[0, 0:nx], below[1, 0:nx], below[2, 0:nx], below[1, 1:nx + 1], down_rows[0], down_rows[1],
            rim_flag[...] == 1, rim[0], rim[1])
        hx, hz = jnp.where(down, hx, 0.0), jnp.where(down, hz, 0.0)
        put_rows(dst, 0, 1, behind, hx)
        put_rows(dst, 2, 1, behind, hz)
        return hx, hz

    def e_update(step, src, h, dst, dst_x, dst_y, comps, p, acc):
        for r in range(0, ny, 8):
            at, below = slice(low + r, low + r + 8), slice(low + r - 1, low + r + 7)
            ps, behind_x = pl.ds(p, BLOCK), pl.ds(p - 1, BLOCK)
            hx, hy, hz = h[0, ps, at], h[1, ps, at], h[2, ps, at]
            keep, gain = ek[behind_x, r:r + 8], eg[behind_x, r:r + 8]
            curls = (
                lambda: (hz - h[2, ps, below]) - (hy - prev_z(hy)),
                lambda: (hx - prev_z(hx)) - (hz - h[2, behind_x, at]),
                lambda: (hy - h[1, behind_x, at]) - (hx - h[0, ps, below]),
            )
            news = {c: keep * src[c, ps, at] + gain * curls[c]() for c in comps}
            for c in comps:
                dst[c, pl.ds(p + dst_x, BLOCK), r + dst_y:r + dst_y + 8] = news[c]
            piece = acc[r // 8]
            for c in (c for c in comps if c < 2):
                for k in range(BLOCK):
                    column = jnp.broadcast_to(news[c][k, :, nz // 2:nz // 2 + 1], (8, nz))
                    piece = jnp.where(lanes(piece) == (step * 2 + c) * nx + p - 1 + k, column, piece)
            acc = acc[:r // 8] + (piece,) + acc[r // 8 + 1:]
        return acc

    loads[3].wait()

    def e_coefficients(p, carry):
        ps = pl.ds(p, BLOCK)
        m = mat[ps]
        absorbs = flag[pl.ds(p + 1, BLOCK), low:high] == 1
        k, g1, g0 = ek1[NMAT - 1], eg1[NMAT - 1], eg0[NMAT - 1]
        for i in range(NMAT - 2, -1, -1):
            here = m == i
            k = jnp.where(here, ek1[i], k)
            g1 = jnp.where(here, eg1[i], g1)
            g0 = jnp.where(here, eg0[i], g0)
        ek[ps] = jnp.where(absorbs, k, 1.0)
        eg[ps] = jnp.where(absorbs, g1, g0)
        return carry

    blocks(0, nx, e_coefficients)
    h_inner(e0, h0, h1)
    wait_recv(round1)
    rim = h_outer(e0, h0, h1, down0, up0, above0, below0, (below0[3, 0:nx], below0[4, 0:nx]))
    rim_h[0], rim_h[1] = rim
    acc = tuple(jnp.zeros((8, nz), jnp.float32) for _ in range(ny // 8))
    step1 = functools.partial(e_update, 0, e0, h1, e1, 0, TOP, (0, 1, 2))
    round2 = e_halo(e1, down1, up1, above1, below1, send2, recv2)
    acc = step1(1, acc)
    acc = step1(nx + 1 - BLOCK, acc)
    start(round2[0:2] + round2[4:6])
    acc = blocks(1 + BLOCK, nx + 1 - BLOCK, step1, acc)
    pack_down(e1, down1)
    pack_up(e1, up1)
    start(round2[2:4])

    h_inner(e1, h1, h2)
    wait_recv(round2)
    h_outer(e1, h1, h2, down1, up1, above1, below1, (rim_h[0], rim_h[1]))
    step2 = functools.partial(e_update, 1, e1, h2, e_out, -1, 0)
    acc = blocks(1, nx + 1, functools.partial(step2, (0, 1)), acc)
    mine = pl.ds(pl.multiple_of(gy * ny, ny), ny)
    samp[mine] = jnp.concatenate(acc, axis=0)
    round3 = []
    for d in range(1, ngy):
        mate = lax.rem(gy + d, ngy)
        copy = pltpu.make_async_remote_copy(
            src_ref=samp.at[mine], dst_ref=samp.at[mine], send_sem=send3.at[d], recv_sem=recv3.at[d],
            device_id=(gx, mate), device_id_type=MESH)
        copy.start()
        round3.append(copy)
    blocks(1, nx + 1, functools.partial(step2, (2,)), acc)
    h_out[...] = h2[:, 1:nx + 1, low:high]
    loads[6].wait()
    slots = 2 * NFREQ // ngy
    rows = lax.broadcasted_iota(jnp.int32, (8, nz), 0)
    angle = jnp.zeros((8, nz), jnp.float32)
    is_cos = jnp.zeros((8, nz), jnp.bool_)
    for n in range(STEPS):
        for k in range(slots):
            here = rows == n * slots + k
            slot = gy * slots + k
            angle = jnp.where(here, omega[lax.rem(slot, NFREQ)] * ((n + 1) * DT), angle)
            is_cos = is_cos | (here & (slot < NFREQ))
    weights[...] = jnp.where(is_cos, jnp.cos(angle), -jnp.sin(angle))
    wait_send(round1)
    wait_send(round2)
    for copy in round3:
        copy.wait_recv()
    for copy in round3:
        copy.wait_send()


def finish(nx, e_in, h_in, samp, weights, e_out, h_out, spectra_out, spectra, sems):
    copies = [
        pltpu.make_async_copy(e_in, e_out, sems.at[0]),
        pltpu.make_async_copy(h_in, h_out, sems.at[1]),
        pltpu.make_async_copy(spectra, spectra_out, sems.at[2]),
    ]
    copies[0].start()
    copies[1].start()
    slots = spectra.shape[0]
    table = samp[...].T
    for k in range(slots):
        for c in range(2):
            total = None
            for n in range(STEPS):
                row = n * slots + k
                coef = weights[row:row + 1, 0:1]
                first = (n * 2 + c) * nx
                term = coef * table[first:first + nx]
                total = term if total is None else total + term
            spectra[k, c] = total
    copies[2].start()
    for copy in copies:
        copy.wait()


def solution(mesh):
    ngx, ngy = mesh.shape["gx"], mesh.shape["gy"]

    def local(electric, magnetic, material, pml_flags, permittivity, pml_sigma, omega):
        _, nx, ny, nz = electric.shape
        slots = 2 * NFREQ // ngy
        hbm = pl.BlockSpec(memory_space=pltpu.HBM)
        vmem = pl.BlockSpec(memory_space=pltpu.VMEM)
        f32 = jnp.float32
        field = jax.ShapeDtypeStruct(electric.shape, f32)
        e_scratch = pltpu.VMEM((3, nx + 2, ny + 16, nz), f32)
        h_scratch = pltpu.VMEM((3, nx + 1, ny + 8, nz), f32)
        operands = (electric, magnetic, material, pml_flags, permittivity, pml_sigma.reshape(1, nz), omega)
        e_done, h_done, samples, weights = pl.pallas_call(
            functools.partial(kernel, ngx, ngy, nx, ny, nz),
            out_shape=(
                pltpu.VMEM(field.shape, f32),
                pltpu.VMEM(field.shape, f32),
                pltpu.VMEM((ngy * ny, nz), f32),
                pltpu.VMEM((8, nz), f32),
            ),
            in_specs=[hbm] * 7,
            out_specs=(vmem, vmem, vmem, vmem),
            scratch_shapes=[
                e_scratch,
                e_scratch,
                h_scratch,
                h_scratch,
                h_scratch,
                pltpu.VMEM((2, nx, nz), f32),
                pltpu.VMEM((2, nx, nz), f32),
                pltpu.VMEM((5, nx, nz), f32),
                pltpu.VMEM((3, nx, nz), f32),
                pltpu.VMEM((2, nx, nz), f32),
                pltpu.VMEM((2, nx, nz), f32),
                pltpu.VMEM((5, nx + 8, nz), f32),
                pltpu.VMEM((3, nx + 8, nz), f32),
                pltpu.VMEM((2, nx, nz), f32),
                pltpu.VMEM((nx, nz), jnp.int32),
                pltpu.VMEM((nx, nz), jnp.int32),
                pltpu.VMEM((nx + 1, ny + 8, nz), jnp.int32),
                pltpu.VMEM((nx, ny, nz), jnp.int32),
                pltpu.VMEM((nx, ny, nz), f32),
                pltpu.VMEM((nx, ny, nz), f32),
                pltpu.SMEM((NMAT,), f32),
                pltpu.VMEM((1, nz), f32),
                pltpu.SMEM((NFREQ,), f32),
                pltpu.SemaphoreType.DMA((7,)),
                pltpu.SemaphoreType.DMA((9,)),
                pltpu.SemaphoreType.DMA((9,)),
                pltpu.SemaphoreType.DMA((6,)),
                pltpu.SemaphoreType.DMA((6,)),
                pltpu.SemaphoreType.DMA((ngy,)),
                pltpu.SemaphoreType.DMA((ngy,)),
            ],
            compiler_params=pltpu.CompilerParams(
                collective_id=0, has_side_effects=True, vmem_limit_bytes=24 * 1024 * 1024),
        )(*[pltpu.with_memory_space_constraint(a, pltpu.HBM) for a in operands])
        spectra = jax.ShapeDtypeStruct((slots, 2, nx, ny * ngy), f32)
        return pl.pallas_call(
            functools.partial(finish, nx),
            out_shape=(field, field, spectra),
            in_specs=[vmem] * 4,
            out_specs=(hbm, hbm, hbm),
            scratch_shapes=[pltpu.VMEM(spectra.shape, f32), pltpu.SemaphoreType.DMA((3,))],
            compiler_params=pltpu.CompilerParams(vmem_limit_bytes=24 * 1024 * 1024),
        )(e_done, h_done, samples, weights)

    placed = (
        P(None, "gx", "gy", None),
        P(None, "gx", "gy", None),
        P("gx", "gy", None),
        P("gx", "gy", None),
        P(),
        P(),
        P(),
    )
    return jax.shard_map(
        local,
        mesh=mesh,
        in_specs=placed,
        out_specs=(P(None, "gx", "gy", None), P(None, "gx", "gy", None), P("gy", None, "gx", None)),
        check_vma=False,
    )
```

```python
import functools

import jax
import jax.numpy as jnp
from jax import lax
from jax.experimental import pallas as pl
from jax.experimental.pallas import tpu as pltpu
from jax.sharding import PartitionSpec as P

STEPS = 2
NFREQ = 8
NMAT = 4
DT = 0.5
MESH = pl.DeviceIdType.MESH

TOP = 8


BLOCK = 4


def blocks(low, high, body, carry=0):
    for p in range(low, high, BLOCK):
        carry = body(p, carry)
    return carry


def kernel(ngx, ngy, nx, ny, nz,
           e_in, h_in, mat_in, flag_in, perm_in, sigma_in, omega_in,
           e_out, h_out, samp, weights,
           e0, e1, h0, h1, h2, down0, down1, up0, up1, above0, above1, below0, below1, rim_h, rim_flag, flag, mat, ek, eg, perm, sigma, omega,
           load_sem, send1, recv1, send2, recv2, send3, recv3):
    gx, gy = lax.axis_index("gx"), lax.axis_index("gy")
    left, right = gx > 0, gx < ngx - 1
    down, up = gy > 0, gy < ngy - 1
    own_x = pl.ds(1, nx)
    own_y = pl.ds(TOP, ny)
    behind, ahead = TOP - 1, TOP + ny
    last = nx + 1

    loads = [
        pltpu.make_async_copy(e_in, e0.at[:, own_x, own_y], load_sem.at[0]),
        pltpu.make_async_copy(h_in, h0.at[:, own_x, own_y], load_sem.at[1]),
        pltpu.make_async_copy(flag_in, flag.at[own_x, own_y], load_sem.at[2]),
        pltpu.make_async_copy(mat_in, mat, load_sem.at[3]),
        pltpu.make_async_copy(sigma_in, sigma, load_sem.at[4]),
        pltpu.make_async_copy(perm_in, perm, load_sem.at[5]),
        pltpu.make_async_copy(omega_in, omega, load_sem.at[6]),
    ]

    barrier = pltpu.get_barrier_semaphore()
    partners = [
        (left, (gx - 1, gy)),
        (right, (gx + 1, gy)),
        (left & up, (gx - 1, gy + 1)),
        (right & down, (gx + 1, gy - 1)),
    ]
    for mate in range(ngy):
        distance = jnp.abs(gy - mate)
        partners.append(((distance == 1) | (distance > 3), (gx, mate)))
    expected = 0
    for there, device in partners:
        expected = expected + there.astype(jnp.int32)

        @pl.when(there)
        def _():
            pl.semaphore_signal(barrier, inc=1, device_id=device, device_id_type=MESH)

    for copy in loads:
        copy.start()

    @pl.when(jnp.logical_not(right))
    def _():
        for e in (e0, e1):
            for c in (1, 2):
                e[c, last, 0:ahead] = jnp.zeros((ahead, nz), jnp.float32)

    @pl.when(jnp.logical_not(up))
    def _():
        for e, above in ((e0, above0), (e1, above1)):
            e[0, 0, ahead:ahead + 8] = jnp.zeros((8, nz), jnp.float32)
            above[...] = jnp.zeros((2, nx, nz), jnp.float32)

    for e in (e0, e1):
        for c in (0, 2):
            e[c, 1:last, ahead:ahead + 8] = jnp.zeros((nx, 8, nz), jnp.float32)

    def row_of(ref, c, first, r):
        planes, rows = ref.shape[-3], ref.shape[-2]
        return pl.ds((c * planes + first) * rows + r, nx, stride=rows)

    def get_rows(ref, c, first, r):
        return ref.reshape(-1, nz)[row_of(ref, c, first, r), :]

    def put_rows(ref, c, first, r, value):
        ref.reshape(-1, nz)[row_of(ref, c, first, r), :] = value

    def pack_down(e, down_rows):
        for i, c in enumerate((0, 2)):
            down_rows[i] = get_rows(e, c, 1, TOP)

    def pack_up(e, up_rows):
        for c in range(3):
            up_rows[c] = get_rows(e, c, 1, TOP + ny - 1)

    pl.semaphore_wait(barrier, expected)

    def remote(src, dst, sends, recvs, i, device):
        return pltpu.make_async_remote_copy(
            src_ref=src, dst_ref=dst, send_sem=sends.at[i], recv_sem=recvs.at[i],
            device_id=device, device_id_type=MESH)

    def e_halo(src, e, above, below, sends, recvs):
        at = functools.partial(remote, sends=sends, recvs=recvs)
        to_left = [at(src["left"], e.at[1:3, last, own_y], i=0, device=(gx - 1, gy))]
        to_right = [at(src["right"], e.at[:, 0, own_y], i=1, device=(gx + 1, gy))]
        to_down = [at(rows, above.at[c], i=2 + c, device=(gx, gy - 1)) for c, rows in enumerate(src["down"])]
        to_up = [at(src["up"], below.at[0:3, 0:nx], i=4, device=(gx, gy + 1))]
        corner_lu = [at(src["left up"], e.at[1, last, behind], i=5, device=(gx - 1, gy + 1))]
        corner_rd = [at(src["right down"], e.at[0, 0, ahead], i=6, device=(gx + 1, gy - 1))]
        return [
            [left, right, to_left],
            [right, left, to_right],
            [down, up, to_down],
            [up, down, to_up],
            [left & up, right & down, corner_lu],
            [right & down, left & up, corner_rd],
        ]

    def start(plan):
        for sends, _, copies in plan:
            @pl.when(sends)
            def _():
                for copy in copies:
                    copy.start()

    def wait_recv(plan):
        for _, receives, copies in plan:
            @pl.when(receives)
            def _():
                for copy in copies:
                    copy.wait_recv()

    def wait_send(plan):
        for sends, _, copies in plan:
            @pl.when(sends)
            def _():
                for copy in copies:
                    copy.wait_send()

    round1 = e_halo({
        "left": e_in.at[1:3, 0],
        "right": e_in.at[:, nx - 1],
        "down": [e_in.at[c, :, 0] for c in (0, 2)],
        "up": e_in.at[:, :, ny - 1],
        "left up": e_in.at[1, 0, ny - 1],
        "right down": e_in.at[0, nx - 1, 0],
    }, e0, above0, below0, send1, recv1)
    at1 = functools.partial(remote, sends=send1, recvs=recv1)
    round1[1][2] += [
        at1(h_in.at[1:3, nx - 1], h0.at[1:3, 0, own_y], i=7, device=(gx + 1, gy)),
        at1(flag_in.at[nx - 1], flag.at[0, own_y], i=8, device=(gx + 1, gy)),
    ]
    round1[3][2] += [
        at1(flag_in.at[:, ny - 1], rim_flag, i=9, device=(gx, gy + 1)),
        at1(h_in.at[0, :, ny - 1], below0.at[3, 0:nx], i=10, device=(gx, gy + 1)),
        at1(h_in.at[2, :, ny - 1], below0.at[4, 0:nx], i=11, device=(gx, gy + 1)),
    ]
    start(round1)
    loads[0].wait()
    loads[1].wait()
    loads[2].wait()
    pack_down(e0, down0)
    pack_up(e0, up0)

    loads[4].wait()
    loads[5].wait()
    sg = sigma[...]
    sm = sg * DT / 2.0
    hk1 = (1.0 - sm) / (1.0 + sm)
    hg1 = DT / (1.0 + sm)
    ek1, eg1, eg0 = [], [], []
    for m in range(NMAT):
        eps = jnp.full((1, nz), perm[m], jnp.float32)
        se = sg * DT / (2.0 * eps)
        ek1.append((1.0 - se) / (1.0 + se))
        eg1.append(DT / (eps * (1.0 + se)))
        eg0.append(DT / eps)

    def lanes(f):
        return lax.broadcasted_iota(jnp.int32, f.shape, f.ndim - 1)

    def next_z(f):
        return jnp.where(lanes(f) == nz - 1, 0.0, pltpu.roll(f, nz - 1, f.ndim - 1))

    def prev_z(f):
        return jnp.where(lanes(f) == 0, 0.0, pltpu.roll(f, 1, f.ndim - 1))

    def h_update(e, src, dst, p, planes, r, n, comps, keep=None):
        at, nxt = slice(r, r + n), slice(r + 1, r + n + 1)
        ps, ahead_x = pl.ds(p, planes), pl.ds(p + 1, planes)
        absorbs = flag[ps, at] == 1
        hk = jnp.where(absorbs, hk1, 1.0)
        hg = jnp.where(absorbs, hg1, DT)
        ex, ey, ez = e[0, ps, at], e[1, ps, at], e[2, ps, at]
        curls = (
            lambda: (e[2, ps, nxt] - ez) - (next_z(ey) - ey),
            lambda: (next_z(ex) - ex) - (e[2, ahead_x, at] - ez),
            lambda: (e[1, ahead_x, at] - ey) - (e[0, ps, nxt] - ex),
        )
        for c in comps:
            new = hk * src[c, ps, at] - hg * curls[c]()
            dst[c, ps, at] = new if keep is None else jnp.where(keep, new, 0.0)

    low, high = TOP, TOP + ny
    inner_end = 1 + (nx - 1) // BLOCK * BLOCK

    def h_inner(e, src, dst):
        def body(p, carry):
            h_update(e, src, dst, p, BLOCK, low, ny, (0, 1, 2))
            return carry
        blocks(1, inner_end, body)

    def h_rows(ex, ey, ez, ey_x, ex_y, ez_y, absorbs, hx, hz):
        hk = jnp.where(absorbs, hk1, 1.0)
        hg = jnp.where(absorbs, hg1, DT)
        return (hk * hx - hg * ((ez_y - ez) - (next_z(ey) - ey)),
                hk * hz - hg * ((ey_x - ey) - (ex_y - ex)))

    def h_outer(e, src, dst, down_rows, up_rows, above, below, rim):
        h_update(e, src, dst, 0, 1, low, ny, (1, 2), left)
        h_update(e, src, dst, inner_end, nx + 1 - inner_end, low, ny, (0, 1, 2))
        r = high - 1
        hx, hz = h_rows(
            up_rows[0], up_rows[1], up_rows[2], get_rows(e, 1, 2, r), above[0], above[1],
            get_rows(flag, 0, 1, r) == 1, get_rows(src, 0, 1, r), get_rows(src, 2, 1, r))
        put_rows(dst, 0, 1, r, hx)
        put_rows(dst, 2, 1, r, hz)
        below[1, nx:nx + 1] = e[1, last, behind:behind + 1]
        hx, hz = h_rows(
            below[0, 0:nx], below[1, 0:nx], below[2, 0:nx], below[1, 1:nx + 1], down_rows[0], down_rows[1],
            rim_flag[...] == 1, rim[0], rim[1])
        hx, hz = jnp.where(down, hx, 0.0), jnp.where(down, hz, 0.0)
        put_rows(dst, 0, 1, behind, hx)
        put_rows(dst, 2, 1, behind, hz)
        return hx, hz

    def e_update(step, src, h, dst, dst_x, dst_y, comps, p, acc):
        for r in range(0, ny, 8):
            at, below = slice(low + r, low + r + 8), slice(low + r - 1, low + r + 7)
            ps, behind_x = pl.ds(p, BLOCK), pl.ds(p - 1, BLOCK)
            hx, hy, hz = h[0, ps, at], h[1, ps, at], h[2, ps, at]
            keep, gain = ek[behind_x, r:r + 8], eg[behind_x, r:r + 8]
            curls = (
                lambda: (hz - h[2, ps, below]) - (hy - prev_z(hy)),
                lambda: (hx - prev_z(hx)) - (hz - h[2, behind_x, at]),
                lambda: (hy - h[1, behind_x, at]) - (hx - h[0, ps, below]),
            )
            news = {c: keep * src[c, ps, at] + gain * curls[c]() for c in comps}
            for c in comps:
                dst[c, pl.ds(p + dst_x, BLOCK), r + dst_y:r + dst_y + 8] = news[c]
            piece = acc[r // 8]
            for c in (c for c in comps if c < 2):
                for k in range(BLOCK):
                    column = jnp.broadcast_to(news[c][k, :, nz // 2:nz // 2 + 1], (8, nz))
                    piece = jnp.where(lanes(piece) == (step * 2 + c) * nx + p - 1 + k, column, piece)
            acc = acc[:r // 8] + (piece,) + acc[r // 8 + 1:]
        return acc

    loads[3].wait()

    def e_coefficients(p, carry):
        ps = pl.ds(p, BLOCK)
        m = mat[ps]
        absorbs = flag[pl.ds(p + 1, BLOCK), low:high] == 1
        k, g1, g0 = ek1[NMAT - 1], eg1[NMAT - 1], eg0[NMAT - 1]
        for i in range(NMAT - 2, -1, -1):
            here = m == i
            k = jnp.where(here, ek1[i], k)
            g1 = jnp.where(here, eg1[i], g1)
            g0 = jnp.where(here, eg0[i], g0)
        ek[ps] = jnp.where(absorbs, k, 1.0)
        eg[ps] = jnp.where(absorbs, g1, g0)
        return carry

    blocks(0, nx, e_coefficients)
    h_inner(e0, h0, h1)
    wait_recv(round1)
    rim = h_outer(e0, h0, h1, down0, up0, above0, below0, (below0[3, 0:nx], below0[4, 0:nx]))
    rim_h[0], rim_h[1] = rim
    acc = tuple(jnp.zeros((8, nz), jnp.float32) for _ in range(ny // 8))
    step1 = functools.partial(e_update, 0, e0, h1, e1, 0, TOP, (0, 1, 2))
    round2 = e_halo({
        "left": e1.at[1:3, 1, own_y],
        "right": e1.at[:, nx, own_y],
        "down": [down1.at[c] for c in range(2)],
        "up": up1,
        "left up": e1.at[1, 1, TOP + ny - 1],
        "right down": e1.at[0, nx, TOP],
    }, e1, above1, below1, send2, recv2)
    acc = step1(1, acc)
    acc = step1(nx + 1 - BLOCK, acc)
    start(round2[0:2] + round2[4:6])
    acc = blocks(1 + BLOCK, nx + 1 - BLOCK, step1, acc)
    pack_down(e1, down1)
    pack_up(e1, up1)
    start(round2[2:4])

    h_inner(e1, h1, h2)
    wait_recv(round2)
    h_outer(e1, h1, h2, down1, up1, above1, below1, (rim_h[0], rim_h[1]))
    step2 = functools.partial(e_update, 1, e1, h2, e_out, -1, 0)
    acc = blocks(1, nx + 1, functools.partial(step2, (0, 1)), acc)
    mine = pl.ds(pl.multiple_of(gy * ny, ny), ny)
    samp[mine] = jnp.concatenate(acc, axis=0)
    round3 = []
    for d in range(1, ngy):
        mate = lax.rem(gy + d, ngy)
        copy = pltpu.make_async_remote_copy(
            src_ref=samp.at[mine], dst_ref=samp.at[mine], send_sem=send3.at[d], recv_sem=recv3.at[d],
            device_id=(gx, mate), device_id_type=MESH)
        copy.start()
        round3.append(copy)
    blocks(1, nx + 1, functools.partial(step2, (2,)), acc)
    h_out[...] = h2[:, 1:nx + 1, low:high]
    loads[6].wait()
    slots = 2 * NFREQ // ngy
    rows = lax.broadcasted_iota(jnp.int32, (8, nz), 0)
    angle = jnp.zeros((8, nz), jnp.float32)
    is_cos = jnp.zeros((8, nz), jnp.bool_)
    for n in range(STEPS):
        for k in range(slots):
            here = rows == n * slots + k
            slot = gy * slots + k
            angle = jnp.where(here, omega[lax.rem(slot, NFREQ)] * ((n + 1) * DT), angle)
            is_cos = is_cos | (here & (slot < NFREQ))
    weights[...] = jnp.where(is_cos, jnp.cos(angle), -jnp.sin(angle))
    wait_send(round1)
    wait_send(round2)
    for copy in round3:
        copy.wait_recv()
    for copy in round3:
        copy.wait_send()


def finish(nx, e_in, h_in, samp, weights, e_out, h_out, spectra_out, spectra, sems):
    copies = [
        pltpu.make_async_copy(e_in, e_out, sems.at[0]),
        pltpu.make_async_copy(h_in, h_out, sems.at[1]),
        pltpu.make_async_copy(spectra, spectra_out, sems.at[2]),
    ]
    copies[0].start()
    copies[1].start()
    slots = spectra.shape[0]
    table = samp[...].T
    for k in range(slots):
        for c in range(2):
            total = None
            for n in range(STEPS):
                row = n * slots + k
                coef = weights[row:row + 1, 0:1]
                first = (n * 2 + c) * nx
                term = coef * table[first:first + nx]
                total = term if total is None else total + term
            spectra[k, c] = total
    copies[2].start()
    for copy in copies:
        copy.wait()


def solution(mesh):
    ngx, ngy = mesh.shape["gx"], mesh.shape["gy"]

    def local(electric, magnetic, material, pml_flags, permittivity, pml_sigma, omega):
        _, nx, ny, nz = electric.shape
        slots = 2 * NFREQ // ngy
        hbm = pl.BlockSpec(memory_space=pltpu.HBM)
        vmem = pl.BlockSpec(memory_space=pltpu.VMEM)
        f32 = jnp.float32
        field = jax.ShapeDtypeStruct(electric.shape, f32)
        e_scratch = pltpu.VMEM((3, nx + 2, ny + 16, nz), f32)
        h_scratch = pltpu.VMEM((3, nx + 1, ny + 8, nz), f32)
        operands = (electric, magnetic, material, pml_flags, permittivity, pml_sigma.reshape(1, nz), omega)
        e_done, h_done, samples, weights = pl.pallas_call(
            functools.partial(kernel, ngx, ngy, nx, ny, nz),
            out_shape=(
                pltpu.VMEM(field.shape, f32),
                pltpu.VMEM(field.shape, f32),
                pltpu.VMEM((ngy * ny, nz), f32),
                pltpu.VMEM((8, nz), f32),
            ),
            in_specs=[hbm] * 7,
            out_specs=(vmem, vmem, vmem, vmem),
            scratch_shapes=[
                e_scratch,
                e_scratch,
                h_scratch,
                h_scratch,
                h_scratch,
                pltpu.VMEM((2, nx, nz), f32),
                pltpu.VMEM((2, nx, nz), f32),
                pltpu.VMEM((3, nx, nz), f32),
                pltpu.VMEM((3, nx, nz), f32),
                pltpu.VMEM((2, nx, nz), f32),
                pltpu.VMEM((2, nx, nz), f32),
                pltpu.VMEM((5, nx + 8, nz), f32),
                pltpu.VMEM((3, nx + 8, nz), f32),
                pltpu.VMEM((2, nx, nz), f32),
                pltpu.VMEM((nx, nz), jnp.int32),
                pltpu.VMEM((nx + 1, ny + 8, nz), jnp.int32),
                pltpu.VMEM((nx, ny, nz), jnp.int32),
                pltpu.VMEM((nx, ny, nz), f32),
                pltpu.VMEM((nx, ny, nz), f32),
                pltpu.SMEM((NMAT,), f32),
                pltpu.VMEM((1, nz), f32),
                pltpu.SMEM((NFREQ,), f32),
                pltpu.SemaphoreType.DMA((7,)),
                pltpu.SemaphoreType.DMA((12,)),
                pltpu.SemaphoreType.DMA((12,)),
                pltpu.SemaphoreType.DMA((7,)),
                pltpu.SemaphoreType.DMA((7,)),
                pltpu.SemaphoreType.DMA((ngy,)),
                pltpu.SemaphoreType.DMA((ngy,)),
            ],
            compiler_params=pltpu.CompilerParams(
                collective_id=0, has_side_effects=True, vmem_limit_bytes=24 * 1024 * 1024),
        )(*[pltpu.with_memory_space_constraint(a, pltpu.HBM) for a in operands])
        spectra = jax.ShapeDtypeStruct((slots, 2, nx, ny * ngy), f32)
        return pl.pallas_call(
            functools.partial(finish, nx),
            out_shape=(field, field, spectra),
            in_specs=[vmem] * 4,
            out_specs=(hbm, hbm, hbm),
            scratch_shapes=[pltpu.VMEM(spectra.shape, f32), pltpu.SemaphoreType.DMA((3,))],
            compiler_params=pltpu.CompilerParams(vmem_limit_bytes=24 * 1024 * 1024),
        )(e_done, h_done, samples, weights)

    placed = (
        P(None, "gx", "gy", None),
        P(None, "gx", "gy", None),
        P("gx", "gy", None),
        P("gx", "gy", None),
        P(),
        P(),
        P(),
    )
    return jax.shard_map(
        local,
        mesh=mesh,
        in_specs=placed,
        out_specs=(P(None, "gx", "gy", None), P(None, "gx", "gy", None), P("gy", None, "gx", None)),
        check_vma=False,
    )
```

```python
import functools

import jax
import jax.numpy as jnp
from jax import lax
from jax.experimental import pallas as pl
from jax.experimental.pallas import tpu as pltpu
from jax.sharding import PartitionSpec as P

STEPS = 2
NFREQ = 8
NMAT = 4
DT = 0.5
MESH = pl.DeviceIdType.MESH

TOP = 8


BLOCK = 4


def blocks(low, high, body, carry=0):
    for p in range(low, high, BLOCK):
        carry = body(p, carry)
    return carry


def kernel(ngx, ngy, nx, ny, nz,
           e_in, h_in, mat_in, flag_in, perm_in, sigma_in, omega_in,
           e_out, h_out, samp, weights,
           e0, e1, h0, h1, h2, down0, down1, up0, up1, above0, above1, below0, below1, rim_h, right0, left0, flag, mat, ek, eg, perm, sigma, omega,
           load_sem, send1, recv1, send2, recv2, send3, recv3):
    gx, gy = lax.axis_index("gx"), lax.axis_index("gy")
    left, right = gx > 0, gx < ngx - 1
    down, up = gy > 0, gy < ngy - 1
    own_x = pl.ds(1, nx)
    own_y = pl.ds(TOP, ny)
    behind, ahead = TOP - 1, TOP + ny
    last = nx + 1

    loads = [
        pltpu.make_async_copy(e_in, e0.at[:, own_x, own_y], load_sem.at[0]),
        pltpu.make_async_copy(h_in, h0.at[:, own_x, own_y], load_sem.at[1]),
        pltpu.make_async_copy(flag_in, flag.at[own_x, own_y], load_sem.at[2]),
        pltpu.make_async_copy(mat_in, mat, load_sem.at[3]),
        pltpu.make_async_copy(sigma_in, sigma, load_sem.at[4]),
        pltpu.make_async_copy(perm_in, perm, load_sem.at[5]),
        pltpu.make_async_copy(omega_in, omega, load_sem.at[6]),
    ]

    barrier = pltpu.get_barrier_semaphore()
    partners = [
        (left, (gx - 1, gy)),
        (right, (gx + 1, gy)),
        (left & up, (gx - 1, gy + 1)),
        (right & down, (gx + 1, gy - 1)),
        (down, (gx, gy - 1)),
        (up, (gx, gy + 1)),
    ]
    if ngy > 4:
        partners += [(jnp.abs(gy - mate) > 3, (gx, mate)) for mate in range(ngy)]
    expected = 0
    for there, device in partners:
        expected = expected + there.astype(jnp.int32)

        @pl.when(there)
        def _():
            pl.semaphore_signal(barrier, inc=1, device_id=device, device_id_type=MESH)

    for copy in loads:
        copy.start()

    @pl.when(jnp.logical_not(right))
    def _():
        for e in (e0, e1):
            for c in (1, 2):
                e[c, last, 0:ahead] = jnp.zeros((ahead, nz), jnp.float32)

    @pl.when(jnp.logical_not(up))
    def _():
        for e, above in ((e0, above0), (e1, above1)):
            e[0, 0, ahead:ahead + 8] = jnp.zeros((8, nz), jnp.float32)
            above[...] = jnp.zeros((2, nx, nz), jnp.float32)

    for e in (e0, e1):
        for c in (0, 2):
            e[c, 1:last, ahead:ahead + 8] = jnp.zeros((nx, 8, nz), jnp.float32)

    def row_of(ref, c, first, r):
        planes, rows = ref.shape[-3], ref.shape[-2]
        return pl.ds((c * planes + first) * rows + r, nx, stride=rows)

    def get_rows(ref, c, first, r):
        return ref.reshape(-1, nz)[row_of(ref, c, first, r), :]

    def put_rows(ref, c, first, r, value):
        ref.reshape(-1, nz)[row_of(ref, c, first, r), :] = value

    def pack_down(e, down_rows):
        for i, c in enumerate((0, 2)):
            down_rows[i] = get_rows(e, c, 1, TOP)

    def pack_up(e, up_rows):
        for c in range(3):
            up_rows[c] = get_rows(e, c, 1, TOP + ny - 1)

    for i in (0, 1, 2):
        loads[i].wait()
    pack_down(e0, down0)
    pack_up(e0, up0)
    for i, c in enumerate((0, 2)):
        up0[3 + i] = get_rows(h0, c, 1, TOP + ny - 1)
    up0[5] = get_rows(flag, 0, 1, TOP + ny - 1).astype(jnp.float32)
    right0[0:3] = e0[:, nx, own_y]
    right0[3:5] = h0[1:3, nx, own_y]
    right0[5] = flag[nx, own_y].astype(jnp.float32)

    pl.semaphore_wait(barrier, expected)

    def remote(src, dst, sends, recvs, i, device):
        return pltpu.make_async_remote_copy(
            src_ref=src, dst_ref=dst, send_sem=sends.at[i], recv_sem=recvs.at[i],
            device_id=device, device_id_type=MESH)

    def e_halo(e, right_planes, behind_planes, down_rows, up_rows, above, below, sends, recvs):
        at = functools.partial(remote, sends=sends, recvs=recvs)
        rim_up = TOP + ny - 1
        to_left = [at(e.at[1:3, 1, own_y], e.at[1:3, last, own_y], i=0, device=(gx - 1, gy))]
        to_right = [at(right_planes, behind_planes, i=1, device=(gx + 1, gy))]
        to_down = [at(down_rows, above, i=2, device=(gx, gy - 1))]
        to_up = [at(up_rows, below.at[:, 0:nx], i=3, device=(gx, gy + 1))]
        corner_lu = [at(e.at[1, 1, rim_up], e.at[1, last, behind], i=4, device=(gx - 1, gy + 1))]
        corner_rd = [at(e.at[0, nx, TOP], e.at[0, 0, ahead], i=5, device=(gx + 1, gy - 1))]
        return [
            [left, right, to_left],
            [right, left, to_right],
            [down, up, to_down],
            [up, down, to_up],
            [left & up, right & down, corner_lu],
            [right & down, left & up, corner_rd],
        ]

    def start(plan):
        for sends, _, copies in plan:
            @pl.when(sends)
            def _():
                for copy in copies:
                    copy.start()

    def wait_recv(plan):
        for _, receives, copies in plan:
            @pl.when(receives)
            def _():
                for copy in copies:
                    copy.wait_recv()

    def wait_send(plan):
        for sends, _, copies in plan:
            @pl.when(sends)
            def _():
                for copy in copies:
                    copy.wait_send()

    round1 = e_halo(e0, right0, left0, down0, up0, above0, below0, send1, recv1)
    start(round1)

    loads[4].wait()
    loads[5].wait()
    sg = sigma[...]
    sm = sg * DT / 2.0
    hk1 = (1.0 - sm) / (1.0 + sm)
    hg1 = DT / (1.0 + sm)
    ek1, eg1, eg0 = [], [], []
    for m in range(NMAT):
        eps = jnp.full((1, nz), perm[m], jnp.float32)
        se = sg * DT / (2.0 * eps)
        ek1.append((1.0 - se) / (1.0 + se))
        eg1.append(DT / (eps * (1.0 + se)))
        eg0.append(DT / eps)

    def lanes(f):
        return lax.broadcasted_iota(jnp.int32, f.shape, f.ndim - 1)

    def next_z(f):
        return jnp.where(lanes(f) == nz - 1, 0.0, pltpu.roll(f, nz - 1, f.ndim - 1))

    def prev_z(f):
        return jnp.where(lanes(f) == 0, 0.0, pltpu.roll(f, 1, f.ndim - 1))

    def h_update(e, src, dst, p, planes, r, n, comps, keep=None):
        at, nxt = slice(r, r + n), slice(r + 1, r + n + 1)
        ps, ahead_x = pl.ds(p, planes), pl.ds(p + 1, planes)
        absorbs = flag[ps, at] == 1
        hk = jnp.where(absorbs, hk1, 1.0)
        hg = jnp.where(absorbs, hg1, DT)
        ex, ey, ez = e[0, ps, at], e[1, ps, at], e[2, ps, at]
        curls = (
            lambda: (e[2, ps, nxt] - ez) - (next_z(ey) - ey),
            lambda: (next_z(ex) - ex) - (e[2, ahead_x, at] - ez),
            lambda: (e[1, ahead_x, at] - ey) - (e[0, ps, nxt] - ex),
        )
        for c in comps:
            new = hk * src[c, ps, at] - hg * curls[c]()
            dst[c, ps, at] = new if keep is None else jnp.where(keep, new, 0.0)

    low, high = TOP, TOP + ny
    inner_end = 1 + (nx - 1) // BLOCK * BLOCK

    def h_inner(e, src, dst):
        def body(p, carry):
            h_update(e, src, dst, p, BLOCK, low, ny, (0, 1, 2))
            return carry
        blocks(1, inner_end, body)

    def h_rows(ex, ey, ez, ey_x, ex_y, ez_y, absorbs, hx, hz):
        hk = jnp.where(absorbs, hk1, 1.0)
        hg = jnp.where(absorbs, hg1, DT)
        return (hk * hx - hg * ((ez_y - ez) - (next_z(ey) - ey)),
                hk * hz - hg * ((ey_x - ey) - (ex_y - ex)))

    def h_outer(e, src, dst, down_rows, up_rows, above, below, rim):
        h_update(e, src, dst, 0, 1, low, ny, (1, 2), left)
        h_update(e, src, dst, inner_end, nx + 1 - inner_end, low, ny, (0, 1, 2))
        r = high - 1
        hx, hz = h_rows(
            up_rows[0], up_rows[1], up_rows[2], get_rows(e, 1, 2, r), above[0], above[1],
            get_rows(flag, 0, 1, r) == 1, get_rows(src, 0, 1, r), get_rows(src, 2, 1, r))
        put_rows(dst, 0, 1, r, hx)
        put_rows(dst, 2, 1, r, hz)
        below[1, nx:nx + 1] = e[1, last, behind:behind + 1]
        hx, hz = h_rows(
            below[0, 0:nx], below[1, 0:nx], below[2, 0:nx], below[1, 1:nx + 1], down_rows[0], down_rows[1],
            below0[5, 0:nx] == 1.0, rim[0], rim[1])
        hx, hz = jnp.where(down, hx, 0.0), jnp.where(down, hz, 0.0)
        put_rows(dst, 0, 1, behind, hx)
        put_rows(dst, 2, 1, behind, hz)
        return hx, hz

    def e_update(step, src, h, dst, dst_x, dst_y, comps, p, acc):
        for r in range(0, ny, 8):
            at, below = slice(low + r, low + r + 8), slice(low + r - 1, low + r + 7)
            ps, behind_x = pl.ds(p, BLOCK), pl.ds(p - 1, BLOCK)
            hx, hy, hz = h[0, ps, at], h[1, ps, at], h[2, ps, at]
            keep, gain = ek[behind_x, r:r + 8], eg[behind_x, r:r + 8]
            curls = (
                lambda: (hz - h[2, ps, below]) - (hy - prev_z(hy)),
                lambda: (hx - prev_z(hx)) - (hz - h[2, behind_x, at]),
                lambda: (hy - h[1, behind_x, at]) - (hx - h[0, ps, below]),
            )
            news = {c: keep * src[c, ps, at] + gain * curls[c]() for c in comps}
            for c in comps:
                dst[c, pl.ds(p + dst_x, BLOCK), r + dst_y:r + dst_y + 8] = news[c]
            piece = acc[r // 8]
            for c in (c for c in comps if c < 2):
                for k in range(BLOCK):
                    column = jnp.broadcast_to(news[c][k, :, nz // 2:nz // 2 + 1], (8, nz))
                    piece = jnp.where(lanes(piece) == (step * 2 + c) * nx + p - 1 + k, column, piece)
            acc = acc[:r // 8] + (piece,) + acc[r // 8 + 1:]
        return acc

    loads[3].wait()

    def e_coefficients(p, carry):
        ps = pl.ds(p, BLOCK)
        m = mat[ps]
        absorbs = flag[pl.ds(p + 1, BLOCK), low:high] == 1
        k, g1, g0 = ek1[NMAT - 1], eg1[NMAT - 1], eg0[NMAT - 1]
        for i in range(NMAT - 2, -1, -1):
            here = m == i
            k = jnp.where(here, ek1[i], k)
            g1 = jnp.where(here, eg1[i], g1)
            g0 = jnp.where(here, eg0[i], g0)
        ek[ps] = jnp.where(absorbs, k, 1.0)
        eg[ps] = jnp.where(absorbs, g1, g0)
        return carry

    blocks(0, nx, e_coefficients)
    h_inner(e0, h0, h1)
    wait_recv(round1)
    e0[:, 0, own_y] = left0[0:3]
    h0[1:3, 0, own_y] = left0[3:5]
    flag[0, own_y] = left0[5].astype(jnp.int32)
    rim = h_outer(e0, h0, h1, down0, up0, above0, below0, (below0[3, 0:nx], below0[4, 0:nx]))
    rim_h[0], rim_h[1] = rim
    acc = tuple(jnp.zeros((8, nz), jnp.float32) for _ in range(ny // 8))
    step1 = functools.partial(e_update, 0, e0, h1, e1, 0, TOP, (0, 1, 2))
    round2 = e_halo(e1, e1.at[:, nx, own_y], e1.at[:, 0, own_y], down1, up1, above1, below1, send2, recv2)
    acc = step1(1, acc)
    acc = step1(nx + 1 - BLOCK, acc)
    start(round2[0:2] + round2[4:6])
    acc = blocks(1 + BLOCK, nx + 1 - BLOCK, step1, acc)
    pack_down(e1, down1)
    pack_up(e1, up1)
    start(round2[2:4])

    h_inner(e1, h1, h2)
    wait_recv(round2)
    h_outer(e1, h1, h2, down1, up1, above1, below1, (rim_h[0], rim_h[1]))
    step2 = functools.partial(e_update, 1, e1, h2, e_out, -1, 0)
    acc = blocks(1, nx + 1, functools.partial(step2, (0, 1)), acc)
    mine = pl.ds(pl.multiple_of(gy * ny, ny), ny)
    samp[mine] = jnp.concatenate(acc, axis=0)
    round3 = []
    for d in range(1, ngy):
        mate = lax.rem(gy + d, ngy)
        copy = pltpu.make_async_remote_copy(
            src_ref=samp.at[mine], dst_ref=samp.at[mine], send_sem=send3.at[d], recv_sem=recv3.at[d],
            device_id=(gx, mate), device_id_type=MESH)
        copy.start()
        round3.append(copy)
    blocks(1, nx + 1, functools.partial(step2, (2,)), acc)
    h_out[...] = h2[:, 1:nx + 1, low:high]
    loads[6].wait()
    slots = 2 * NFREQ // ngy
    rows = lax.broadcasted_iota(jnp.int32, (8, nz), 0)
    angle = jnp.zeros((8, nz), jnp.float32)
    is_cos = jnp.zeros((8, nz), jnp.bool_)
    for n in range(STEPS):
        for k in range(slots):
            here = rows == n * slots + k
            slot = gy * slots + k
            angle = jnp.where(here, omega[lax.rem(slot, NFREQ)] * ((n + 1) * DT), angle)
            is_cos = is_cos | (here & (slot < NFREQ))
    weights[...] = jnp.where(is_cos, jnp.cos(angle), -jnp.sin(angle))
    wait_send(round1)
    wait_send(round2)
    for copy in round3:
        copy.wait_recv()
    for copy in round3:
        copy.wait_send()


def finish(nx, e_in, h_in, samp, weights, e_out, h_out, spectra_out, spectra, sems):
    copies = [
        pltpu.make_async_copy(e_in, e_out, sems.at[0]),
        pltpu.make_async_copy(h_in, h_out, sems.at[1]),
        pltpu.make_async_copy(spectra, spectra_out, sems.at[2]),
    ]
    copies[0].start()
    copies[1].start()
    slots = spectra.shape[0]
    table = samp[...].T
    for k in range(slots):
        for c in range(2):
            total = None
            for n in range(STEPS):
                row = n * slots + k
                coef = weights[row:row + 1, 0:1]
                first = (n * 2 + c) * nx
                term = coef * table[first:first + nx]
                total = term if total is None else total + term
            spectra[k, c] = total
    copies[2].start()
    for copy in copies:
        copy.wait()


def solution(mesh):
    ngx, ngy = mesh.shape["gx"], mesh.shape["gy"]

    def local(electric, magnetic, material, pml_flags, permittivity, pml_sigma, omega):
        _, nx, ny, nz = electric.shape
        slots = 2 * NFREQ // ngy
        hbm = pl.BlockSpec(memory_space=pltpu.HBM)
        vmem = pl.BlockSpec(memory_space=pltpu.VMEM)
        f32 = jnp.float32
        field = jax.ShapeDtypeStruct(electric.shape, f32)
        e_scratch = pltpu.VMEM((3, nx + 2, ny + 16, nz), f32)
        h_scratch = pltpu.VMEM((3, nx + 1, ny + 8, nz), f32)
        operands = (electric, magnetic, material, pml_flags, permittivity, pml_sigma.reshape(1, nz), omega)
        e_done, h_done, samples, weights = pl.pallas_call(
            functools.partial(kernel, ngx, ngy, nx, ny, nz),
            out_shape=(
                pltpu.VMEM(field.shape, f32),
                pltpu.VMEM(field.shape, f32),
                pltpu.VMEM((ngy * ny, nz), f32),
                pltpu.VMEM((8, nz), f32),
            ),
            in_specs=[hbm] * 7,
            out_specs=(vmem, vmem, vmem, vmem),
            scratch_shapes=[
                e_scratch,
                e_scratch,
                h_scratch,
                h_scratch,
                h_scratch,
                pltpu.VMEM((2, nx, nz), f32),
                pltpu.VMEM((2, nx, nz), f32),
                pltpu.VMEM((6, nx, nz), f32),
                pltpu.VMEM((3, nx, nz), f32),
                pltpu.VMEM((2, nx, nz), f32),
                pltpu.VMEM((2, nx, nz), f32),
                pltpu.VMEM((6, nx + 8, nz), f32),
                pltpu.VMEM((3, nx + 8, nz), f32),
                pltpu.VMEM((2, nx, nz), f32),
                pltpu.VMEM((6, ny, nz), f32),
                pltpu.VMEM((6, ny, nz), f32),
                pltpu.VMEM((nx + 1, ny + 8, nz), jnp.int32),
                pltpu.VMEM((nx, ny, nz), jnp.int32),
                pltpu.VMEM((nx, ny, nz), f32),
                pltpu.VMEM((nx, ny, nz), f32),
                pltpu.SMEM((NMAT,), f32),
                pltpu.VMEM((1, nz), f32),
                pltpu.SMEM((NFREQ,), f32),
                pltpu.SemaphoreType.DMA((7,)),
                pltpu.SemaphoreType.DMA((6,)),
                pltpu.SemaphoreType.DMA((6,)),
                pltpu.SemaphoreType.DMA((6,)),
                pltpu.SemaphoreType.DMA((6,)),
                pltpu.SemaphoreType.DMA((ngy,)),
                pltpu.SemaphoreType.DMA((ngy,)),
            ],
            compiler_params=pltpu.CompilerParams(
                collective_id=0, has_side_effects=True, vmem_limit_bytes=24 * 1024 * 1024),
        )(*[pltpu.with_memory_space_constraint(a, pltpu.HBM) for a in operands])
        spectra = jax.ShapeDtypeStruct((slots, 2, nx, ny * ngy), f32)
        return pl.pallas_call(
            functools.partial(finish, nx),
            out_shape=(field, field, spectra),
            in_specs=[vmem] * 4,
            out_specs=(hbm, hbm, hbm),
            scratch_shapes=[pltpu.VMEM(spectra.shape, f32), pltpu.SemaphoreType.DMA((3,))],
            compiler_params=pltpu.CompilerParams(vmem_limit_bytes=24 * 1024 * 1024),
        )(e_done, h_done, samples, weights)

    placed = (
        P(None, "gx", "gy", None),
        P(None, "gx", "gy", None),
        P("gx", "gy", None),
        P("gx", "gy", None),
        P(),
        P(),
        P(),
    )
    return jax.shard_map(
        local,
        mesh=mesh,
        in_specs=placed,
        out_specs=(P(None, "gx", "gy", None), P(None, "gx", "gy", None), P("gy", None, "gx", None)),
        check_vma=False,
    )
```

```python
import functools

import jax
import jax.numpy as jnp
from jax import lax
from jax.experimental import pallas as pl
from jax.experimental.pallas import tpu as pltpu
from jax.sharding import PartitionSpec as P

STEPS = 2
NFREQ = 8
NMAT = 4
DT = 0.5
MESH = pl.DeviceIdType.MESH

TOP = 8


BLOCK = 4


def blocks(low, high, body, carry=0):
    for p in range(low, high, BLOCK):
        carry = body(p, carry)
    return carry


def kernel(ngx, ngy, nx, ny, nz,
           e_in, h_in, mat_in, flag_in, perm_in, sigma_in, omega_in,
           e_out, h_out, samp, weights,
           e0, e1, h0, h1, h2, down0, down1, up0, up1, above0, above1, below0, below1, rim_h, right0, left0, flag, mat, ek, eg, perm, sigma, omega,
           load_sem, send1, recv1, send2, recv2, send3, recv3):
    gx, gy = lax.axis_index("gx"), lax.axis_index("gy")
    left, right = gx > 0, gx < ngx - 1
    down, up = gy > 0, gy < ngy - 1
    own_x = pl.ds(1, nx)
    own_y = pl.ds(TOP, ny)
    behind, ahead = TOP - 1, TOP + ny
    last = nx + 1

    loads = [
        pltpu.make_async_copy(e_in, e0.at[:, own_x, own_y], load_sem.at[0]),
        pltpu.make_async_copy(h_in, h0.at[:, own_x, own_y], load_sem.at[1]),
        pltpu.make_async_copy(flag_in, flag.at[own_x, own_y], load_sem.at[2]),
        pltpu.make_async_copy(mat_in, mat, load_sem.at[3]),
        pltpu.make_async_copy(sigma_in, sigma, load_sem.at[4]),
        pltpu.make_async_copy(perm_in, perm, load_sem.at[5]),
        pltpu.make_async_copy(omega_in, omega, load_sem.at[6]),
    ]

    barrier = pltpu.get_barrier_semaphore()
    partners = [
        (left, (gx - 1, gy)),
        (right, (gx + 1, gy)),
        (left & up, (gx - 1, gy + 1)),
        (right & down, (gx + 1, gy - 1)),
        (down, (gx, gy - 1)),
        (up, (gx, gy + 1)),
    ]
    if ngy > 4:
        partners += [(jnp.abs(gy - mate) > 3, (gx, mate)) for mate in range(ngy)]
    expected = 0
    for there, device in partners:
        expected = expected + there.astype(jnp.int32)

        @pl.when(there)
        def _():
            pl.semaphore_signal(barrier, inc=1, device_id=device, device_id_type=MESH)

    for copy in loads:
        copy.start()

    @pl.when(jnp.logical_not(right))
    def _():
        for e in (e0, e1):
            for c in (1, 2):
                e[c, last, 0:ahead] = jnp.zeros((ahead, nz), jnp.float32)

    @pl.when(jnp.logical_not(up))
    def _():
        for e, above in ((e0, above0), (e1, above1)):
            e[0, 0, ahead:ahead + 8] = jnp.zeros((8, nz), jnp.float32)
            above[...] = jnp.zeros((2, nx, nz), jnp.float32)

    for e in (e0, e1):
        for c in (0, 2):
            e[c, 1:last, ahead:ahead + 8] = jnp.zeros((nx, 8, nz), jnp.float32)

    def row_of(ref, c, first, r):
        planes, rows = ref.shape[-3], ref.shape[-2]
        return pl.ds((c * planes + first) * rows + r, nx, stride=rows)

    def get_rows(ref, c, first, r):
        return ref.reshape(-1, nz)[row_of(ref, c, first, r), :]

    def put_rows(ref, c, first, r, value):
        ref.reshape(-1, nz)[row_of(ref, c, first, r), :] = value

    def pack_down(e, down_rows):
        for i, c in enumerate((0, 2)):
            down_rows[i] = get_rows(e, c, 1, TOP)

    def pack_up(e, up_rows):
        for c in range(3):
            up_rows[c] = get_rows(e, c, 1, TOP + ny - 1)

    for i in (0, 1, 2):
        loads[i].wait()
    pack_down(e0, down0)
    pack_up(e0, up0)
    for i, c in enumerate((0, 2)):
        up0[3 + i] = get_rows(h0, c, 1, TOP + ny - 1)
    up0[5] = get_rows(flag, 0, 1, TOP + ny - 1).astype(jnp.float32)
    right0[0:3] = e0[:, nx, own_y]
    right0[3:5] = h0[1:3, nx, own_y]
    right0[5] = flag[nx, own_y].astype(jnp.float32)

    pl.semaphore_wait(barrier, expected)

    def remote(src, dst, sends, recvs, i, device):
        return pltpu.make_async_remote_copy(
            src_ref=src, dst_ref=dst, send_sem=sends.at[i], recv_sem=recvs.at[i],
            device_id=device, device_id_type=MESH)

    def e_halo(e, right_planes, behind_planes, down_rows, up_rows, above, below, sends, recvs):
        at = functools.partial(remote, sends=sends, recvs=recvs)
        to_left = [at(e.at[1:3, 1, own_y], e.at[1:3, last, own_y], i=0, device=(gx - 1, gy))]
        to_right = [at(right_planes, behind_planes, i=1, device=(gx + 1, gy))]
        to_down = [at(down_rows, above, i=2, device=(gx, gy - 1))]
        to_up = [at(up_rows, below.at[:, 0:nx], i=3, device=(gx, gy + 1))]
        corner_lu = [at(up_rows.at[1, 0], e.at[1, last, behind], i=4, device=(gx - 1, gy + 1))]
        corner_rd = [at(down_rows.at[0, nx - 1], e.at[0, 0, ahead], i=5, device=(gx + 1, gy - 1))]
        return [
            [left, right, to_left],
            [right, left, to_right],
            [down, up, to_down],
            [up, down, to_up],
            [left & up, right & down, corner_lu],
            [right & down, left & up, corner_rd],
        ]

    def start(plan):
        for sends, _, copies in plan:
            @pl.when(sends)
            def _():
                for copy in copies:
                    copy.start()

    def wait_recv(plan):
        for _, receives, copies in plan:
            @pl.when(receives)
            def _():
                for copy in copies:
                    copy.wait_recv()

    def wait_send(plan):
        for sends, _, copies in plan:
            @pl.when(sends)
            def _():
                for copy in copies:
                    copy.wait_send()

    round1 = e_halo(e0, right0, left0, down0, up0, above0, below0, send1, recv1)
    start(round1[4:6] + round1[0:4])

    loads[4].wait()
    loads[5].wait()
    sg = sigma[...]
    sm = sg * DT / 2.0
    hk1 = (1.0 - sm) / (1.0 + sm)
    hg1 = DT / (1.0 + sm)
    ek1, eg1, eg0 = [], [], []
    for m in range(NMAT):
        eps = jnp.full((1, nz), perm[m], jnp.float32)
        se = sg * DT / (2.0 * eps)
        ek1.append((1.0 - se) / (1.0 + se))
        eg1.append(DT / (eps * (1.0 + se)))
        eg0.append(DT / eps)

    def lanes(f):
        return lax.broadcasted_iota(jnp.int32, f.shape, f.ndim - 1)

    def next_z(f):
        return jnp.where(lanes(f) == nz - 1, 0.0, pltpu.roll(f, nz - 1, f.ndim - 1))

    def prev_z(f):
        return jnp.where(lanes(f) == 0, 0.0, pltpu.roll(f, 1, f.ndim - 1))

    def h_update(e, src, dst, p, planes, r, n, comps, keep=None):
        at, nxt = slice(r, r + n), slice(r + 1, r + n + 1)
        ps, ahead_x = pl.ds(p, planes), pl.ds(p + 1, planes)
        absorbs = flag[ps, at] == 1
        hk = jnp.where(absorbs, hk1, 1.0)
        hg = jnp.where(absorbs, hg1, DT)
        ex, ey, ez = e[0, ps, at], e[1, ps, at], e[2, ps, at]
        curls = (
            lambda: (e[2, ps, nxt] - ez) - (next_z(ey) - ey),
            lambda: (next_z(ex) - ex) - (e[2, ahead_x, at] - ez),
            lambda: (e[1, ahead_x, at] - ey) - (e[0, ps, nxt] - ex),
        )
        for c in comps:
            new = hk * src[c, ps, at] - hg * curls[c]()
            dst[c, ps, at] = new if keep is None else jnp.where(keep, new, 0.0)

    low, high = TOP, TOP + ny
    inner_end = 1 + (nx - 1) // BLOCK * BLOCK

    def h_inner(e, src, dst):
        def body(p, carry):
            h_update(e, src, dst, p, BLOCK, low, ny, (0, 1, 2))
            return carry
        blocks(1, inner_end, body)

    def h_rows(ex, ey, ez, ey_x, ex_y, ez_y, absorbs, hx, hz):
        hk = jnp.where(absorbs, hk1, 1.0)
        hg = jnp.where(absorbs, hg1, DT)
        return (hk * hx - hg * ((ez_y - ez) - (next_z(ey) - ey)),
                hk * hz - hg * ((ey_x - ey) - (ex_y - ex)))

    def h_outer(e, src, dst, down_rows, up_rows, above, below, rim):
        h_update(e, src, dst, 0, 1, low, ny, (1, 2), left)
        h_update(e, src, dst, inner_end, nx + 1 - inner_end, low, ny, (0, 1, 2))
        r = high - 1
        hx, hz = h_rows(
            up_rows[0], up_rows[1], up_rows[2], get_rows(e, 1, 2, r), above[0], above[1],
            get_rows(flag, 0, 1, r) == 1, get_rows(src, 0, 1, r), get_rows(src, 2, 1, r))
        put_rows(dst, 0, 1, r, hx)
        put_rows(dst, 2, 1, r, hz)
        below[1, nx:nx + 1] = e[1, last, behind:behind + 1]
        hx, hz = h_rows(
            below[0, 0:nx], below[1, 0:nx], below[2, 0:nx], below[1, 1:nx + 1], down_rows[0], down_rows[1],
            below0[5, 0:nx] == 1.0, rim[0], rim[1])
        hx, hz = jnp.where(down, hx, 0.0), jnp.where(down, hz, 0.0)
        put_rows(dst, 0, 1, behind, hx)
        put_rows(dst, 2, 1, behind, hz)
        return hx, hz

    def e_update(step, src, h, dst, dst_x, dst_y, comps, p, acc):
        for r in range(0, ny, 8):
            at, below = slice(low + r, low + r + 8), slice(low + r - 1, low + r + 7)
            ps, behind_x = pl.ds(p, BLOCK), pl.ds(p - 1, BLOCK)
            hx, hy, hz = h[0, ps, at], h[1, ps, at], h[2, ps, at]
            keep, gain = ek[behind_x, r:r + 8], eg[behind_x, r:r + 8]
            curls = (
                lambda: (hz - h[2, ps, below]) - (hy - prev_z(hy)),
                lambda: (hx - prev_z(hx)) - (hz - h[2, behind_x, at]),
                lambda: (hy - h[1, behind_x, at]) - (hx - h[0, ps, below]),
            )
            news = {c: keep * src[c, ps, at] + gain * curls[c]() for c in comps}
            for c in comps:
                dst[c, pl.ds(p + dst_x, BLOCK), r + dst_y:r + dst_y + 8] = news[c]
            piece = acc[r // 8]
            for c in (c for c in comps if c < 2):
                for k in range(BLOCK):
                    column = jnp.broadcast_to(news[c][k, :, nz // 2:nz // 2 + 1], (8, nz))
                    piece = jnp.where(lanes(piece) == (step * 2 + c) * nx + p - 1 + k, column, piece)
            acc = acc[:r // 8] + (piece,) + acc[r // 8 + 1:]
        return acc

    loads[3].wait()

    def e_coefficients(p, carry):
        ps = pl.ds(p, BLOCK)
        m = mat[ps]
        absorbs = flag[pl.ds(p + 1, BLOCK), low:high] == 1
        k, g1, g0 = ek1[NMAT - 1], eg1[NMAT - 1], eg0[NMAT - 1]
        for i in range(NMAT - 2, -1, -1):
            here = m == i
            k = jnp.where(here, ek1[i], k)
            g1 = jnp.where(here, eg1[i], g1)
            g0 = jnp.where(here, eg0[i], g0)
        ek[ps] = jnp.where(absorbs, k, 1.0)
        eg[ps] = jnp.where(absorbs, g1, g0)
        return carry

    blocks(0, nx, e_coefficients)
    h_inner(e0, h0, h1)
    wait_recv(round1)
    e0[:, 0, own_y] = left0[0:3]
    h0[1:3, 0, own_y] = left0[3:5]
    flag[0, own_y] = left0[5].astype(jnp.int32)
    rim = h_outer(e0, h0, h1, down0, up0, above0, below0, (below0[3, 0:nx], below0[4, 0:nx]))
    rim_h[0], rim_h[1] = rim
    acc = tuple(jnp.zeros((8, nz), jnp.float32) for _ in range(ny // 8))
    step1 = functools.partial(e_update, 0, e0, h1, e1, 0, TOP, (0, 1, 2))
    round2 = e_halo(e1, e1.at[:, nx, own_y], e1.at[:, 0, own_y], down1, up1, above1, below1, send2, recv2)

    def e_rows(y, comps, out):
        r = TOP + y
        hx, hy, hz = (get_rows(h1, c, 1, r) for c in range(3))
        keep, gain = get_rows(ek, 0, 0, y), get_rows(eg, 0, 0, y)
        curls = (
            lambda: (hz - get_rows(h1, 2, 1, r - 1)) - (hy - prev_z(hy)),
            lambda: (hx - prev_z(hx)) - (hz - get_rows(h1, 2, 0, r)),
            lambda: (hy - get_rows(h1, 1, 0, r)) - (hx - get_rows(h1, 0, 1, r - 1)),
        )
        for i, c in enumerate(comps):
            out[i] = keep * get_rows(e0, c, 1, r) + gain * curls[c]()

    e_rows(ny - 1, (0, 1, 2), up1)
    e_rows(0, (0, 2), down1)
    start(round2[4:6] + round2[2:4])
    acc = step1(1, acc)
    acc = step1(nx + 1 - BLOCK, acc)
    start(round2[0:2])
    acc = blocks(1 + BLOCK, nx + 1 - BLOCK, step1, acc)

    h_inner(e1, h1, h2)
    wait_recv(round2)
    h_outer(e1, h1, h2, down1, up1, above1, below1, (rim_h[0], rim_h[1]))
    step2 = functools.partial(e_update, 1, e1, h2, e_out, -1, 0)
    acc = blocks(1, nx + 1, functools.partial(step2, (0, 1)), acc)
    mine = pl.ds(pl.multiple_of(gy * ny, ny), ny)
    samp[mine] = jnp.concatenate(acc, axis=0)
    round3 = []
    for d in range(1, ngy):
        mate = lax.rem(gy + d, ngy)
        copy = pltpu.make_async_remote_copy(
            src_ref=samp.at[mine], dst_ref=samp.at[mine], send_sem=send3.at[d], recv_sem=recv3.at[d],
            device_id=(gx, mate), device_id_type=MESH)
        copy.start()
        round3.append(copy)
    blocks(1, nx + 1, functools.partial(step2, (2,)), acc)
    h_out[...] = h2[:, 1:nx + 1, low:high]
    loads[6].wait()
    slots = 2 * NFREQ // ngy
    rows = lax.broadcasted_iota(jnp.int32, (8, nz), 0)
    angle = jnp.zeros((8, nz), jnp.float32)
    is_cos = jnp.zeros((8, nz), jnp.bool_)
    for n in range(STEPS):
        for k in range(slots):
            here = rows == n * slots + k
            slot = gy * slots + k
            angle = jnp.where(here, omega[lax.rem(slot, NFREQ)] * ((n + 1) * DT), angle)
            is_cos = is_cos | (here & (slot < NFREQ))
    weights[...] = jnp.where(is_cos, jnp.cos(angle), -jnp.sin(angle))
    wait_send(round1)
    wait_send(round2)
    for copy in round3:
        copy.wait_recv()
    for copy in round3:
        copy.wait_send()


def finish(nx, e_in, h_in, samp, weights, e_out, h_out, spectra_out, spectra, sems):
    copies = [
        pltpu.make_async_copy(e_in, e_out, sems.at[0]),
        pltpu.make_async_copy(h_in, h_out, sems.at[1]),
        pltpu.make_async_copy(spectra, spectra_out, sems.at[2]),
    ]
    copies[0].start()
    copies[1].start()
    slots = spectra.shape[0]
    table = samp[...].T
    for k in range(slots):
        for c in range(2):
            total = None
            for n in range(STEPS):
                row = n * slots + k
                coef = weights[row:row + 1, 0:1]
                first = (n * 2 + c) * nx
                term = coef * table[first:first + nx]
                total = term if total is None else total + term
            spectra[k, c] = total
    copies[2].start()
    for copy in copies:
        copy.wait()


def solution(mesh):
    ngx, ngy = mesh.shape["gx"], mesh.shape["gy"]

    def local(electric, magnetic, material, pml_flags, permittivity, pml_sigma, omega):
        _, nx, ny, nz = electric.shape
        slots = 2 * NFREQ // ngy
        hbm = pl.BlockSpec(memory_space=pltpu.HBM)
        vmem = pl.BlockSpec(memory_space=pltpu.VMEM)
        f32 = jnp.float32
        field = jax.ShapeDtypeStruct(electric.shape, f32)
        e_scratch = pltpu.VMEM((3, nx + 2, ny + 16, nz), f32)
        h_scratch = pltpu.VMEM((3, nx + 1, ny + 8, nz), f32)
        operands = (electric, magnetic, material, pml_flags, permittivity, pml_sigma.reshape(1, nz), omega)
        e_done, h_done, samples, weights = pl.pallas_call(
            functools.partial(kernel, ngx, ngy, nx, ny, nz),
            out_shape=(
                pltpu.VMEM(field.shape, f32),
                pltpu.VMEM(field.shape, f32),
                pltpu.VMEM((ngy * ny, nz), f32),
                pltpu.VMEM((8, nz), f32),
            ),
            in_specs=[hbm] * 7,
            out_specs=(vmem, vmem, vmem, vmem),
            scratch_shapes=[
                e_scratch,
                e_scratch,
                h_scratch,
                h_scratch,
                h_scratch,
                pltpu.VMEM((2, nx, nz), f32),
                pltpu.VMEM((2, nx, nz), f32),
                pltpu.VMEM((6, nx, nz), f32),
                pltpu.VMEM((3, nx, nz), f32),
                pltpu.VMEM((2, nx, nz), f32),
                pltpu.VMEM((2, nx, nz), f32),
                pltpu.VMEM((6, nx + 8, nz), f32),
                pltpu.VMEM((3, nx + 8, nz), f32),
                pltpu.VMEM((2, nx, nz), f32),
                pltpu.VMEM((6, ny, nz), f32),
                pltpu.VMEM((6, ny, nz), f32),
                pltpu.VMEM((nx + 1, ny + 8, nz), jnp.int32),
                pltpu.VMEM((nx, ny, nz), jnp.int32),
                pltpu.VMEM((nx, ny, nz), f32),
                pltpu.VMEM((nx, ny, nz), f32),
                pltpu.SMEM((NMAT,), f32),
                pltpu.VMEM((1, nz), f32),
                pltpu.SMEM((NFREQ,), f32),
                pltpu.SemaphoreType.DMA((7,)),
                pltpu.SemaphoreType.DMA((6,)),
                pltpu.SemaphoreType.DMA((6,)),
                pltpu.SemaphoreType.DMA((6,)),
                pltpu.SemaphoreType.DMA((6,)),
                pltpu.SemaphoreType.DMA((ngy,)),
                pltpu.SemaphoreType.DMA((ngy,)),
            ],
            compiler_params=pltpu.CompilerParams(
                collective_id=0, has_side_effects=True, vmem_limit_bytes=24 * 1024 * 1024),
        )(*[pltpu.with_memory_space_constraint(a, pltpu.HBM) for a in operands])
        spectra = jax.ShapeDtypeStruct((slots, 2, nx, ny * ngy), f32)
        return pl.pallas_call(
            functools.partial(finish, nx),
            out_shape=(field, field, spectra),
            in_specs=[vmem] * 4,
            out_specs=(hbm, hbm, hbm),
            scratch_shapes=[pltpu.VMEM(spectra.shape, f32), pltpu.SemaphoreType.DMA((3,))],
            compiler_params=pltpu.CompilerParams(vmem_limit_bytes=24 * 1024 * 1024),
        )(e_done, h_done, samples, weights)

    placed = (
        P(None, "gx", "gy", None),
        P(None, "gx", "gy", None),
        P("gx", "gy", None),
        P("gx", "gy", None),
        P(),
        P(),
        P(),
    )
    return jax.shard_map(
        local,
        mesh=mesh,
        in_specs=placed,
        out_specs=(P(None, "gx", "gy", None), P(None, "gx", "gy", None), P("gy", None, "gx", None)),
        check_vma=False,
    )
```

```python
import functools

import jax
import jax.numpy as jnp
from jax import lax
from jax.experimental import pallas as pl
from jax.experimental.pallas import tpu as pltpu
from jax.sharding import PartitionSpec as P

STEPS = 2
NFREQ = 8
NMAT = 4
DT = 0.5
MESH = pl.DeviceIdType.MESH

TOP = 8


BLOCK = 4


def blocks(low, high, body, carry=0):
    pairs = (high - low) // (2 * BLOCK)

    def pair(i, carry):
        p = low + i * (2 * BLOCK)
        return body(p + BLOCK, body(p, carry))

    carry = lax.fori_loop(0, pairs, pair, carry)
    for p in range(low + pairs * 2 * BLOCK, high, BLOCK):
        carry = body(p, carry)
    return carry


def kernel(ngx, ngy, nx, ny, nz,
           e_in, h_in, mat_in, flag_in, perm_in, sigma_in, omega_in,
           e_out, h_out, samp, weights,
           e0, e1, h0, h1, h2, down0, down1, up0, up1, above0, above1, below0, below1, rim_h, right0, left0, flag, mat, ek, eg, perm, sigma, omega,
           load_sem, send1, recv1, send2, recv2, send3, recv3):
    gx, gy = lax.axis_index("gx"), lax.axis_index("gy")
    left, right = gx > 0, gx < ngx - 1
    down, up = gy > 0, gy < ngy - 1
    own_x = pl.ds(1, nx)
    own_y = pl.ds(TOP, ny)
    behind, ahead = TOP - 1, TOP + ny
    last = nx + 1

    loads = [
        pltpu.make_async_copy(e_in, e0.at[:, own_x, own_y], load_sem.at[0]),
        pltpu.make_async_copy(h_in, h0.at[:, own_x, own_y], load_sem.at[1]),
        pltpu.make_async_copy(flag_in, flag.at[own_x, own_y], load_sem.at[2]),
        pltpu.make_async_copy(mat_in, mat, load_sem.at[3]),
        pltpu.make_async_copy(sigma_in, sigma, load_sem.at[4]),
        pltpu.make_async_copy(perm_in, perm, load_sem.at[5]),
        pltpu.make_async_copy(omega_in, omega, load_sem.at[6]),
    ]

    barrier = pltpu.get_barrier_semaphore()
    partners = [
        (left, (gx - 1, gy)),
        (right, (gx + 1, gy)),
        (left & up, (gx - 1, gy + 1)),
        (right & down, (gx + 1, gy - 1)),
        (down, (gx, gy - 1)),
        (up, (gx, gy + 1)),
    ]
    if ngy > 4:
        partners += [(jnp.abs(gy - mate) > 3, (gx, mate)) for mate in range(ngy)]
    expected = 0
    for there, device in partners:
        expected = expected + there.astype(jnp.int32)

        @pl.when(there)
        def _():
            pl.semaphore_signal(barrier, inc=1, device_id=device, device_id_type=MESH)

    for copy in loads:
        copy.start()

    @pl.when(jnp.logical_not(right))
    def _():
        for e in (e0, e1):
            for c in (1, 2):
                e[c, last, 0:ahead] = jnp.zeros((ahead, nz), jnp.float32)

    @pl.when(jnp.logical_not(up))
    def _():
        for e, above in ((e0, above0), (e1, above1)):
            e[0, 0, ahead:ahead + 8] = jnp.zeros((8, nz), jnp.float32)
            above[...] = jnp.zeros((2, nx, nz), jnp.float32)

    for e in (e0, e1):
        for c in (0, 2):
            e[c, 1:last, ahead:ahead + 8] = jnp.zeros((nx, 8, nz), jnp.float32)

    def row_of(ref, c, first, r):
        planes, rows = ref.shape[-3], ref.shape[-2]
        return pl.ds((c * planes + first) * rows + r, nx, stride=rows)

    def get_rows(ref, c, first, r):
        return ref.reshape(-1, nz)[row_of(ref, c, first, r), :]

    def put_rows(ref, c, first, r, value):
        ref.reshape(-1, nz)[row_of(ref, c, first, r), :] = value

    def pack_down(e, down_rows):
        for i, c in enumerate((0, 2)):
            down_rows[i] = get_rows(e, c, 1, TOP)

    def pack_up(e, up_rows):
        for c in range(3):
            up_rows[c] = get_rows(e, c, 1, TOP + ny - 1)

    for i in (0, 1, 2):
        loads[i].wait()
    pack_down(e0, down0)
    pack_up(e0, up0)
    for i, c in enumerate((0, 2)):
        up0[3 + i] = get_rows(h0, c, 1, TOP + ny - 1)
    up0[5] = get_rows(flag, 0, 1, TOP + ny - 1).astype(jnp.float32)
    right0[0:3] = e0[:, nx, own_y]
    right0[3:5] = h0[1:3, nx, own_y]
    right0[5] = flag[nx, own_y].astype(jnp.float32)

    pl.semaphore_wait(barrier, expected)

    def remote(src, dst, sends, recvs, i, device):
        return pltpu.make_async_remote_copy(
            src_ref=src, dst_ref=dst, send_sem=sends.at[i], recv_sem=recvs.at[i],
            device_id=device, device_id_type=MESH)

    def e_halo(e, right_planes, behind_planes, down_rows, up_rows, above, below, sends, recvs):
        at = functools.partial(remote, sends=sends, recvs=recvs)
        to_left = [at(e.at[1:3, 1, own_y], e.at[1:3, last, own_y], i=0, device=(gx - 1, gy))]
        to_right = [at(right_planes, behind_planes, i=1, device=(gx + 1, gy))]
        to_down = [at(down_rows, above, i=2, device=(gx, gy - 1))]
        to_up = [at(up_rows, below.at[:, 0:nx], i=3, device=(gx, gy + 1))]
        corner_lu = [at(up_rows.at[1, 0], e.at[1, last, behind], i=4, device=(gx - 1, gy + 1))]
        corner_rd = [at(down_rows.at[0, nx - 1], e.at[0, 0, ahead], i=5, device=(gx + 1, gy - 1))]
        return [
            [left, right, to_left],
            [right, left, to_right],
            [down, up, to_down],
            [up, down, to_up],
            [left & up, right & down, corner_lu],
            [right & down, left & up, corner_rd],
        ]

    def start(plan):
        for sends, _, copies in plan:
            @pl.when(sends)
            def _():
                for copy in copies:
                    copy.start()

    def wait_recv(plan):
        for _, receives, copies in plan:
            @pl.when(receives)
            def _():
                for copy in copies:
                    copy.wait_recv()

    def wait_send(plan):
        for sends, _, copies in plan:
            @pl.when(sends)
            def _():
                for copy in copies:
                    copy.wait_send()

    round1 = e_halo(e0, right0, left0, down0, up0, above0, below0, send1, recv1)
    start(round1[4:6] + round1[0:4])

    loads[4].wait()
    loads[5].wait()
    sg = sigma[...]
    sm = sg * DT / 2.0
    hk1 = (1.0 - sm) / (1.0 + sm)
    hg1 = DT / (1.0 + sm)
    ek1, eg1, eg0 = [], [], []
    for m in range(NMAT):
        eps = jnp.full((1, nz), perm[m], jnp.float32)
        se = sg * DT / (2.0 * eps)
        ek1.append((1.0 - se) / (1.0 + se))
        eg1.append(DT / (eps * (1.0 + se)))
        eg0.append(DT / eps)

    def lanes(f):
        return lax.broadcasted_iota(jnp.int32, f.shape, f.ndim - 1)

    def next_z(f):
        return jnp.where(lanes(f) == nz - 1, 0.0, pltpu.roll(f, nz - 1, f.ndim - 1))

    def prev_z(f):
        return jnp.where(lanes(f) == 0, 0.0, pltpu.roll(f, 1, f.ndim - 1))

    def h_update(e, src, dst, p, planes, r, n, comps, keep=None):
        at, nxt = slice(r, r + n), slice(r + 1, r + n + 1)
        ps, ahead_x = pl.ds(p, planes), pl.ds(p + 1, planes)
        absorbs = flag[ps, at] == 1
        hk = jnp.where(absorbs, hk1, 1.0)
        hg = jnp.where(absorbs, hg1, DT)
        ex, ey, ez = e[0, ps, at], e[1, ps, at], e[2, ps, at]
        curls = (
            lambda: (e[2, ps, nxt] - ez) - (next_z(ey) - ey),
            lambda: (next_z(ex) - ex) - (e[2, ahead_x, at] - ez),
            lambda: (e[1, ahead_x, at] - ey) - (e[0, ps, nxt] - ex),
        )
        for c in comps:
            new = hk * src[c, ps, at] - hg * curls[c]()
            dst[c, ps, at] = new if keep is None else jnp.where(keep, new, 0.0)

    low, high = TOP, TOP + ny
    inner_end = 1 + (nx - 1) // BLOCK * BLOCK

    def h_inner(e, src, dst):
        def body(p, carry):
            h_update(e, src, dst, p, BLOCK, low, ny, (0, 1, 2))
            return carry
        blocks(1, inner_end, body)

    def h_rows(ex, ey, ez, ey_x, ex_y, ez_y, absorbs, hx, hz):
        hk = jnp.where(absorbs, hk1, 1.0)
        hg = jnp.where(absorbs, hg1, DT)
        return (hk * hx - hg * ((ez_y - ez) - (next_z(ey) - ey)),
                hk * hz - hg * ((ey_x - ey) - (ex_y - ex)))

    def h_outer(e, src, dst, down_rows, up_rows, above, below, rim):
        h_update(e, src, dst, 0, 1, low, ny, (1, 2), left)
        h_update(e, src, dst, inner_end, nx + 1 - inner_end, low, ny, (0, 1, 2))
        r = high - 1
        hx, hz = h_rows(
            up_rows[0], up_rows[1], up_rows[2], get_rows(e, 1, 2, r), above[0], above[1],
            get_rows(flag, 0, 1, r) == 1, get_rows(src, 0, 1, r), get_rows(src, 2, 1, r))
        put_rows(dst, 0, 1, r, hx)
        put_rows(dst, 2, 1, r, hz)
        below[1, nx:nx + 1] = e[1, last, behind:behind + 1]
        hx, hz = h_rows(
            below[0, 0:nx], below[1, 0:nx], below[2, 0:nx], below[1, 1:nx + 1], down_rows[0], down_rows[1],
            below0[5, 0:nx] == 1.0, rim[0], rim[1])
        hx, hz = jnp.where(down, hx, 0.0), jnp.where(down, hz, 0.0)
        put_rows(dst, 0, 1, behind, hx)
        put_rows(dst, 2, 1, behind, hz)
        return hx, hz

    def e_update(step, src, h, dst, dst_x, dst_y, comps, p, acc):
        for r in range(0, ny, 8):
            at, below = slice(low + r, low + r + 8), slice(low + r - 1, low + r + 7)
            ps, behind_x = pl.ds(p, BLOCK), pl.ds(p - 1, BLOCK)
            hx, hy, hz = h[0, ps, at], h[1, ps, at], h[2, ps, at]
            keep, gain = ek[behind_x, r:r + 8], eg[behind_x, r:r + 8]
            curls = (
                lambda: (hz - h[2, ps, below]) - (hy - prev_z(hy)),
                lambda: (hx - prev_z(hx)) - (hz - h[2, behind_x, at]),
                lambda: (hy - h[1, behind_x, at]) - (hx - h[0, ps, below]),
            )
            news = {c: keep * src[c, ps, at] + gain * curls[c]() for c in comps}
            for c in comps:
                dst[c, pl.ds(p + dst_x, BLOCK), r + dst_y:r + dst_y + 8] = news[c]
            piece = acc[r // 8]
            for c in (c for c in comps if c < 2):
                for k in range(BLOCK):
                    column = jnp.broadcast_to(news[c][k, :, nz // 2:nz // 2 + 1], (8, nz))
                    piece = jnp.where(lanes(piece) == (step * 2 + c) * nx + p - 1 + k, column, piece)
            acc = acc[:r // 8] + (piece,) + acc[r // 8 + 1:]
        return acc

    loads[3].wait()

    def e_coefficients(p, carry):
        ps = pl.ds(p, BLOCK)
        m = mat[ps]
        absorbs = flag[pl.ds(p + 1, BLOCK), low:high] == 1
        k, g1, g0 = ek1[NMAT - 1], eg1[NMAT - 1], eg0[NMAT - 1]
        for i in range(NMAT - 2, -1, -1):
            here = m == i
            k = jnp.where(here, ek1[i], k)
            g1 = jnp.where(here, eg1[i], g1)
            g0 = jnp.where(here, eg0[i], g0)
        ek[ps] = jnp.where(absorbs, k, 1.0)
        eg[ps] = jnp.where(absorbs, g1, g0)
        return carry

    blocks(0, nx, e_coefficients)
    h_inner(e0, h0, h1)
    wait_recv(round1)
    e0[:, 0, own_y] = left0[0:3]
    h0[1:3, 0, own_y] = left0[3:5]
    flag[0, own_y] = left0[5].astype(jnp.int32)
    rim = h_outer(e0, h0, h1, down0, up0, above0, below0, (below0[3, 0:nx], below0[4, 0:nx]))
    rim_h[0], rim_h[1] = rim
    acc = tuple(jnp.zeros((8, nz), jnp.float32) for _ in range(ny // 8))
    step1 = functools.partial(e_update, 0, e0, h1, e1, 0, TOP, (0, 1, 2))
    round2 = e_halo(e1, e1.at[:, nx, own_y], e1.at[:, 0, own_y], down1, up1, above1, below1, send2, recv2)

    def e_rows(y, comps, out):
        r = TOP + y
        hx, hy, hz = (get_rows(h1, c, 1, r) for c in range(3))
        keep, gain = get_rows(ek, 0, 0, y), get_rows(eg, 0, 0, y)
        curls = (
            lambda: (hz - get_rows(h1, 2, 1, r - 1)) - (hy - prev_z(hy)),
            lambda: (hx - prev_z(hx)) - (hz - get_rows(h1, 2, 0, r)),
            lambda: (hy - get_rows(h1, 1, 0, r)) - (hx - get_rows(h1, 0, 1, r - 1)),
        )
        for i, c in enumerate(comps):
            out[i] = keep * get_rows(e0, c, 1, r) + gain * curls[c]()

    e_rows(ny - 1, (0, 1, 2), up1)
    e_rows(0, (0, 2), down1)
    start(round2[4:6] + round2[2:4])
    acc = step1(1, acc)
    acc = step1(nx + 1 - BLOCK, acc)
    start(round2[0:2])
    acc = blocks(1 + BLOCK, nx + 1 - BLOCK, step1, acc)

    h_inner(e1, h1, h2)
    wait_recv(round2)
    h_outer(e1, h1, h2, down1, up1, above1, below1, (rim_h[0], rim_h[1]))
    step2 = functools.partial(e_update, 1, e1, h2, e_out, -1, 0)
    acc = blocks(1, nx + 1, functools.partial(step2, (0, 1)), acc)
    mine = pl.ds(pl.multiple_of(gy * ny, ny), ny)
    samp[mine] = jnp.concatenate(acc, axis=0)
    round3 = []
    for d in range(1, ngy):
        mate = lax.rem(gy + d, ngy)
        copy = pltpu.make_async_remote_copy(
            src_ref=samp.at[mine], dst_ref=samp.at[mine], send_sem=send3.at[d], recv_sem=recv3.at[d],
            device_id=(gx, mate), device_id_type=MESH)
        copy.start()
        round3.append(copy)
    blocks(1, nx + 1, functools.partial(step2, (2,)), acc)
    h_out[...] = h2[:, 1:nx + 1, low:high]
    loads[6].wait()
    slots = 2 * NFREQ // ngy
    rows = lax.broadcasted_iota(jnp.int32, (8, nz), 0)
    angle = jnp.zeros((8, nz), jnp.float32)
    is_cos = jnp.zeros((8, nz), jnp.bool_)
    for n in range(STEPS):
        for k in range(slots):
            here = rows == n * slots + k
            slot = gy * slots + k
            angle = jnp.where(here, omega[lax.rem(slot, NFREQ)] * ((n + 1) * DT), angle)
            is_cos = is_cos | (here & (slot < NFREQ))
    weights[...] = jnp.where(is_cos, jnp.cos(angle), -jnp.sin(angle))
    wait_send(round1)
    wait_send(round2)
    for copy in round3:
        copy.wait_recv()
    for copy in round3:
        copy.wait_send()


def finish(nx, e_in, h_in, samp, weights, e_out, h_out, spectra_out, spectra, sems):
    copies = [
        pltpu.make_async_copy(e_in, e_out, sems.at[0]),
        pltpu.make_async_copy(h_in, h_out, sems.at[1]),
        pltpu.make_async_copy(spectra, spectra_out, sems.at[2]),
    ]
    copies[0].start()
    copies[1].start()
    slots = spectra.shape[0]
    table = samp[...].T
    for k in range(slots):
        for c in range(2):
            total = None
            for n in range(STEPS):
                row = n * slots + k
                coef = weights[row:row + 1, 0:1]
                first = (n * 2 + c) * nx
                term = coef * table[first:first + nx]
                total = term if total is None else total + term
            spectra[k, c] = total
    copies[2].start()
    for copy in copies:
        copy.wait()


def solution(mesh):
    ngx, ngy = mesh.shape["gx"], mesh.shape["gy"]

    def local(electric, magnetic, material, pml_flags, permittivity, pml_sigma, omega):
        _, nx, ny, nz = electric.shape
        slots = 2 * NFREQ // ngy
        hbm = pl.BlockSpec(memory_space=pltpu.HBM)
        vmem = pl.BlockSpec(memory_space=pltpu.VMEM)
        f32 = jnp.float32
        field = jax.ShapeDtypeStruct(electric.shape, f32)
        e_scratch = pltpu.VMEM((3, nx + 2, ny + 16, nz), f32)
        h_scratch = pltpu.VMEM((3, nx + 1, ny + 8, nz), f32)
        operands = (electric, magnetic, material, pml_flags, permittivity, pml_sigma.reshape(1, nz), omega)
        e_done, h_done, samples, weights = pl.pallas_call(
            functools.partial(kernel, ngx, ngy, nx, ny, nz),
            out_shape=(
                pltpu.VMEM(field.shape, f32),
                pltpu.VMEM(field.shape, f32),
                pltpu.VMEM((ngy * ny, nz), f32),
                pltpu.VMEM((8, nz), f32),
            ),
            in_specs=[hbm] * 7,
            out_specs=(vmem, vmem, vmem, vmem),
            scratch_shapes=[
                e_scratch,
                e_scratch,
                h_scratch,
                h_scratch,
                h_scratch,
                pltpu.VMEM((2, nx, nz), f32),
                pltpu.VMEM((2, nx, nz), f32),
                pltpu.VMEM((6, nx, nz), f32),
                pltpu.VMEM((3, nx, nz), f32),
                pltpu.VMEM((2, nx, nz), f32),
                pltpu.VMEM((2, nx, nz), f32),
                pltpu.VMEM((6, nx + 8, nz), f32),
                pltpu.VMEM((3, nx + 8, nz), f32),
                pltpu.VMEM((2, nx, nz), f32),
                pltpu.VMEM((6, ny, nz), f32),
                pltpu.VMEM((6, ny, nz), f32),
                pltpu.VMEM((nx + 1, ny + 8, nz), jnp.int32),
                pltpu.VMEM((nx, ny, nz), jnp.int32),
                pltpu.VMEM((nx, ny, nz), f32),
                pltpu.VMEM((nx, ny, nz), f32),
                pltpu.SMEM((NMAT,), f32),
                pltpu.VMEM((1, nz), f32),
                pltpu.SMEM((NFREQ,), f32),
                pltpu.SemaphoreType.DMA((7,)),
                pltpu.SemaphoreType.DMA((6,)),
                pltpu.SemaphoreType.DMA((6,)),
                pltpu.SemaphoreType.DMA((6,)),
                pltpu.SemaphoreType.DMA((6,)),
                pltpu.SemaphoreType.DMA((ngy,)),
                pltpu.SemaphoreType.DMA((ngy,)),
            ],
            compiler_params=pltpu.CompilerParams(
                collective_id=0, has_side_effects=True, vmem_limit_bytes=24 * 1024 * 1024),
        )(*[pltpu.with_memory_space_constraint(a, pltpu.HBM) for a in operands])
        spectra = jax.ShapeDtypeStruct((slots, 2, nx, ny * ngy), f32)
        return pl.pallas_call(
            functools.partial(finish, nx),
            out_shape=(field, field, spectra),
            in_specs=[vmem] * 4,
            out_specs=(hbm, hbm, hbm),
            scratch_shapes=[pltpu.VMEM(spectra.shape, f32), pltpu.SemaphoreType.DMA((3,))],
            compiler_params=pltpu.CompilerParams(vmem_limit_bytes=24 * 1024 * 1024),
        )(e_done, h_done, samples, weights)

    placed = (
        P(None, "gx", "gy", None),
        P(None, "gx", "gy", None),
        P("gx", "gy", None),
        P("gx", "gy", None),
        P(),
        P(),
        P(),
    )
    return jax.shard_map(
        local,
        mesh=mesh,
        in_specs=placed,
        out_specs=(P(None, "gx", "gy", None), P(None, "gx", "gy", None), P("gy", None, "gx", None)),
        check_vma=False,
    )
```

```python
import functools

import jax
import jax.numpy as jnp
from jax import lax
from jax.experimental import pallas as pl
from jax.experimental.pallas import tpu as pltpu
from jax.sharding import PartitionSpec as P

STEPS = 2
NFREQ = 8
NMAT = 4
DT = 0.5
MESH = pl.DeviceIdType.MESH

TOP = 8


BLOCK = 4


def blocks(low, high, body, carry=0):
    rounds = (high - low) // BLOCK
    carry = lax.fori_loop(0, rounds, lambda i, c: body(low + i * BLOCK, c), carry)
    rest = low + rounds * BLOCK
    if rest < high:
        carry = body(rest, carry, high - rest)
    return carry


def kernel(ngx, ngy, nx, ny, nz,
           e_in, h_in, mat_in, flag_in, perm_in, sigma_in, omega_in,
           e_out, h_out, samp, weights,
           e0, e1, h0, h1, h2, down0, down1, up0, up1, above0, above1, below0, below1, rim_h, right0, left0, flag, mat, ek, eg, perm, sigma, omega,
           load_sem, send1, recv1, send2, recv2, send3, recv3):
    gx, gy = lax.axis_index("gx"), lax.axis_index("gy")
    left, right = gx > 0, gx < ngx - 1
    down, up = gy > 0, gy < ngy - 1
    own_x = pl.ds(1, nx)
    own_y = pl.ds(TOP, ny)
    behind, ahead = TOP - 1, TOP + ny
    last = nx + 1

    loads = [
        pltpu.make_async_copy(e_in, e0.at[:, own_x, own_y], load_sem.at[0]),
        pltpu.make_async_copy(h_in, h0.at[:, own_x, own_y], load_sem.at[1]),
        pltpu.make_async_copy(flag_in, flag.at[own_x, own_y], load_sem.at[2]),
        pltpu.make_async_copy(mat_in, mat, load_sem.at[3]),
        pltpu.make_async_copy(sigma_in, sigma, load_sem.at[4]),
        pltpu.make_async_copy(perm_in, perm, load_sem.at[5]),
        pltpu.make_async_copy(omega_in, omega, load_sem.at[6]),
    ]

    barrier = pltpu.get_barrier_semaphore()
    partners = [
        (left, (gx - 1, gy)),
        (right, (gx + 1, gy)),
        (left & up, (gx - 1, gy + 1)),
        (right & down, (gx + 1, gy - 1)),
        (down, (gx, gy - 1)),
        (up, (gx, gy + 1)),
    ]
    if ngy > 4:
        partners += [(jnp.abs(gy - mate) > 3, (gx, mate)) for mate in range(ngy)]
    expected = 0
    for there, device in partners:
        expected = expected + there.astype(jnp.int32)

        @pl.when(there)
        def _():
            pl.semaphore_signal(barrier, inc=1, device_id=device, device_id_type=MESH)

    for copy in loads:
        copy.start()

    @pl.when(jnp.logical_not(right))
    def _():
        for e in (e0, e1):
            for c in (1, 2):
                e[c, last, 0:ahead] = jnp.zeros((ahead, nz), jnp.float32)

    @pl.when(jnp.logical_not(up))
    def _():
        for e, above in ((e0, above0), (e1, above1)):
            e[0, 0, ahead:ahead + 8] = jnp.zeros((8, nz), jnp.float32)
            above[...] = jnp.zeros((2, nx, nz), jnp.float32)

    def row_of(ref, c, first, r):
        planes, rows = ref.shape[-3], ref.shape[-2]
        return pl.ds((c * planes + first) * rows + r, nx, stride=rows)

    def get_rows(ref, c, first, r):
        return ref.reshape(-1, nz)[row_of(ref, c, first, r), :]

    def put_rows(ref, c, first, r, value):
        ref.reshape(-1, nz)[row_of(ref, c, first, r), :] = value

    def pack_down(e, down_rows):
        for i, c in enumerate((0, 2)):
            down_rows[i] = get_rows(e, c, 1, TOP)

    def pack_up(e, up_rows):
        for c in range(3):
            up_rows[c] = get_rows(e, c, 1, TOP + ny - 1)

    for i in (0, 1, 2):
        loads[i].wait()
    pack_down(e0, down0)
    pack_up(e0, up0)
    for i, c in enumerate((0, 2)):
        up0[3 + i] = get_rows(h0, c, 1, TOP + ny - 1)
    up0[5] = get_rows(flag, 0, 1, TOP + ny - 1).astype(jnp.float32)
    right0[0:3] = e0[:, nx, own_y]
    right0[3:5] = h0[1:3, nx, own_y]
    right0[5] = flag[nx, own_y].astype(jnp.float32)

    pl.semaphore_wait(barrier, expected)

    def remote(src, dst, sends, recvs, i, device):
        return pltpu.make_async_remote_copy(
            src_ref=src, dst_ref=dst, send_sem=sends.at[i], recv_sem=recvs.at[i],
            device_id=device, device_id_type=MESH)

    def e_halo(e, right_planes, behind_planes, down_rows, up_rows, above, below, sends, recvs):
        at = functools.partial(remote, sends=sends, recvs=recvs)
        to_left = [at(e.at[1:3, 1, own_y], e.at[1:3, last, own_y], i=0, device=(gx - 1, gy))]
        to_right = [at(right_planes, behind_planes, i=1, device=(gx + 1, gy))]
        to_down = [at(down_rows, above, i=2, device=(gx, gy - 1))]
        to_up = [at(up_rows, below.at[:, 0:nx], i=3, device=(gx, gy + 1))]
        corner_lu = [at(up_rows.at[1, 0], e.at[1, last, behind], i=4, device=(gx - 1, gy + 1))]
        corner_rd = [at(down_rows.at[0, nx - 1], e.at[0, 0, ahead], i=5, device=(gx + 1, gy - 1))]
        return [
            [left, right, to_left],
            [right, left, to_right],
            [down, up, to_down],
            [up, down, to_up],
            [left & up, right & down, corner_lu],
            [right & down, left & up, corner_rd],
        ]

    def start(plan):
        for sends, _, copies in plan:
            @pl.when(sends)
            def _():
                for copy in copies:
                    copy.start()

    def wait_recv(plan):
        for _, receives, copies in plan:
            @pl.when(receives)
            def _():
                for copy in copies:
                    copy.wait_recv()

    def wait_send(plan):
        for sends, _, copies in plan:
            @pl.when(sends)
            def _():
                for copy in copies:
                    copy.wait_send()

    round1 = e_halo(e0, right0, left0, down0, up0, above0, below0, send1, recv1)
    start(round1[4:6] + round1[0:4])

    loads[4].wait()
    loads[5].wait()
    sg = sigma[...]
    sm = sg * DT / 2.0
    hk1 = (1.0 - sm) / (1.0 + sm)
    hg1 = DT / (1.0 + sm)
    ek1, eg1, eg0 = [], [], []
    for m in range(NMAT):
        eps = jnp.full((1, nz), perm[m], jnp.float32)
        se = sg * DT / (2.0 * eps)
        ek1.append((1.0 - se) / (1.0 + se))
        eg1.append(DT / (eps * (1.0 + se)))
        eg0.append(DT / eps)

    def lanes(f):
        return lax.broadcasted_iota(jnp.int32, f.shape, f.ndim - 1)

    def next_z(f):
        return jnp.where(lanes(f) == nz - 1, 0.0, pltpu.roll(f, nz - 1, f.ndim - 1))

    def prev_z(f):
        return jnp.where(lanes(f) == 0, 0.0, pltpu.roll(f, 1, f.ndim - 1))

    def h_update(e, src, dst, p, planes, r, n, comps, keep=None):
        at, nxt = slice(r, r + n), slice(r + 1, r + n + 1)
        ps, ahead_x = pl.ds(p, planes), pl.ds(p + 1, planes)
        absorbs = flag[ps, at] == 1
        hk = jnp.where(absorbs, hk1, 1.0)
        hg = jnp.where(absorbs, hg1, DT)
        ex, ey, ez = e[0, ps, at], e[1, ps, at], e[2, ps, at]
        curls = (
            lambda: (e[2, ps, nxt] - ez) - (next_z(ey) - ey),
            lambda: (next_z(ex) - ex) - (e[2, ahead_x, at] - ez),
            lambda: (e[1, ahead_x, at] - ey) - (e[0, ps, nxt] - ex),
        )
        for c in comps:
            new = hk * src[c, ps, at] - hg * curls[c]()
            dst[c, ps, at] = new if keep is None else jnp.where(keep, new, 0.0)

    low, high = TOP, TOP + ny
    inner_end = 1 + (nx - 1) // BLOCK * BLOCK

    def h_inner(e, src, dst):
        def body(p, carry, planes=BLOCK):
            h_update(e, src, dst, p, planes, low, ny, (0, 1, 2))
            return carry
        blocks(1, inner_end, body)

    def h_rows(ex, ey, ez, ey_x, ex_y, ez_y, absorbs, hx, hz):
        hk = jnp.where(absorbs, hk1, 1.0)
        hg = jnp.where(absorbs, hg1, DT)
        return (hk * hx - hg * ((ez_y - ez) - (next_z(ey) - ey)),
                hk * hz - hg * ((ey_x - ey) - (ex_y - ex)))

    def h_outer(e, src, dst, down_rows, up_rows, above, below, rim):
        h_update(e, src, dst, 0, 1, low, ny, (1, 2), left)
        h_update(e, src, dst, inner_end, nx + 1 - inner_end, low, ny, (0, 1, 2))
        r = high - 1
        hx, hz = h_rows(
            up_rows[0], up_rows[1], up_rows[2], get_rows(e, 1, 2, r), above[0], above[1],
            get_rows(flag, 0, 1, r) == 1, get_rows(src, 0, 1, r), get_rows(src, 2, 1, r))
        put_rows(dst, 0, 1, r, hx)
        put_rows(dst, 2, 1, r, hz)
        below[1, nx:nx + 1] = e[1, last, behind:behind + 1]
        hx, hz = h_rows(
            below[0, 0:nx], below[1, 0:nx], below[2, 0:nx], below[1, 1:nx + 1], down_rows[0], down_rows[1],
            below0[5, 0:nx] == 1.0, rim[0], rim[1])
        hx, hz = jnp.where(down, hx, 0.0), jnp.where(down, hz, 0.0)
        put_rows(dst, 0, 1, behind, hx)
        put_rows(dst, 2, 1, behind, hz)
        return hx, hz

    def e_update(step, src, h, dst, dst_x, dst_y, comps, p, acc, planes=BLOCK):
        for r in range(0, ny, 8):
            at, below = slice(low + r, low + r + 8), slice(low + r - 1, low + r + 7)
            ps, behind_x = pl.ds(p, planes), pl.ds(p - 1, planes)
            hx, hy, hz = h[0, ps, at], h[1, ps, at], h[2, ps, at]
            keep, gain = ek[behind_x, r:r + 8], eg[behind_x, r:r + 8]
            curls = (
                lambda: (hz - h[2, ps, below]) - (hy - prev_z(hy)),
                lambda: (hx - prev_z(hx)) - (hz - h[2, behind_x, at]),
                lambda: (hy - h[1, behind_x, at]) - (hx - h[0, ps, below]),
            )
            news = {c: keep * src[c, ps, at] + gain * curls[c]() for c in comps}
            for c in comps:
                dst[c, pl.ds(p + dst_x, planes), r + dst_y:r + dst_y + 8] = news[c]
            piece = acc[r // 8]
            for c in (c for c in comps if c < 2):
                for k in range(planes):
                    column = jnp.broadcast_to(news[c][k, :, nz // 2:nz // 2 + 1], (8, nz))
                    piece = jnp.where(lanes(piece) == (step * 2 + c) * nx + p - 1 + k, column, piece)
            acc = acc[:r // 8] + (piece,) + acc[r // 8 + 1:]
        return acc

    loads[3].wait()

    def e_coefficients(p, carry):
        ps = pl.ds(p, BLOCK)
        m = mat[ps]
        absorbs = flag[pl.ds(p + 1, BLOCK), low:high] == 1
        k, g1, g0 = ek1[NMAT - 1], eg1[NMAT - 1], eg0[NMAT - 1]
        for i in range(NMAT - 2, -1, -1):
            here = m == i
            k = jnp.where(here, ek1[i], k)
            g1 = jnp.where(here, eg1[i], g1)
            g0 = jnp.where(here, eg0[i], g0)
        ek[ps] = jnp.where(absorbs, k, 1.0)
        eg[ps] = jnp.where(absorbs, g1, g0)
        return carry

    blocks(0, nx, e_coefficients)
    h_inner(e0, h0, h1)
    wait_recv(round1)
    e0[:, 0, own_y] = left0[0:3]
    h0[1:3, 0, own_y] = left0[3:5]
    flag[0, own_y] = left0[5].astype(jnp.int32)
    rim = h_outer(e0, h0, h1, down0, up0, above0, below0, (below0[3, 0:nx], below0[4, 0:nx]))
    rim_h[0], rim_h[1] = rim
    acc = tuple(jnp.zeros((8, nz), jnp.float32) for _ in range(ny // 8))
    step1 = functools.partial(e_update, 0, e0, h1, e1, 0, TOP, (0, 1, 2))
    round2 = e_halo(e1, e1.at[:, nx, own_y], e1.at[:, 0, own_y], down1, up1, above1, below1, send2, recv2)

    def e_rows(y, comps, out):
        r = TOP + y
        hx, hy, hz = (get_rows(h1, c, 1, r) for c in range(3))
        keep, gain = get_rows(ek, 0, 0, y), get_rows(eg, 0, 0, y)
        curls = (
            lambda: (hz - get_rows(h1, 2, 1, r - 1)) - (hy - prev_z(hy)),
            lambda: (hx - prev_z(hx)) - (hz - get_rows(h1, 2, 0, r)),
            lambda: (hy - get_rows(h1, 1, 0, r)) - (hx - get_rows(h1, 0, 1, r - 1)),
        )
        for i, c in enumerate(comps):
            out[i] = keep * get_rows(e0, c, 1, r) + gain * curls[c]()

    acc = step1(1, acc, 1)
    acc = step1(nx, acc, 1)
    start(round2[0:2])
    e_rows(ny - 1, (0, 1, 2), up1)
    e_rows(0, (0, 2), down1)
    start(round2[4:6] + round2[2:4])
    acc = blocks(2, nx, step1, acc)

    h_inner(e1, h1, h2)
    wait_recv(round2)
    h_outer(e1, h1, h2, down1, up1, above1, below1, (rim_h[0], rim_h[1]))
    h_copy = pltpu.make_async_copy(h2.at[:, own_x, own_y], h_out, load_sem.at[7])
    h_copy.start()
    step2 = functools.partial(e_update, 1, e1, h2, e_out, -1, 0)
    acc = blocks(1, nx + 1, functools.partial(step2, (0, 1)), acc)
    mine = pl.ds(pl.multiple_of(gy * ny, ny), ny)
    samp[mine] = jnp.concatenate(acc, axis=0)
    round3 = []
    for d in range(1, ngy):
        mate = lax.rem(gy + d, ngy)
        copy = pltpu.make_async_remote_copy(
            src_ref=samp.at[mine], dst_ref=samp.at[mine], send_sem=send3.at[d], recv_sem=recv3.at[d],
            device_id=(gx, mate), device_id_type=MESH)
        copy.start()
        round3.append(copy)
    blocks(1, nx + 1, functools.partial(step2, (2,)), acc)
    loads[6].wait()
    slots = 2 * NFREQ // ngy
    rows = lax.broadcasted_iota(jnp.int32, (8, nz), 0)
    angle = jnp.zeros((8, nz), jnp.float32)
    is_cos = jnp.zeros((8, nz), jnp.bool_)
    for n in range(STEPS):
        for k in range(slots):
            here = rows == n * slots + k
            slot = gy * slots + k
            angle = jnp.where(here, omega[lax.rem(slot, NFREQ)] * ((n + 1) * DT), angle)
            is_cos = is_cos | (here & (slot < NFREQ))
    weights[...] = jnp.where(is_cos, jnp.cos(angle), -jnp.sin(angle))
    wait_send(round1)
    wait_send(round2)
    for copy in round3:
        copy.wait_recv()
    for copy in round3:
        copy.wait_send()
    h_copy.wait()


def finish(nx, e_in, h_in, samp, weights, e_out, h_out, spectra_out, spectra, sems):
    copies = [
        pltpu.make_async_copy(e_in, e_out, sems.at[0]),
        pltpu.make_async_copy(h_in, h_out, sems.at[1]),
        pltpu.make_async_copy(spectra, spectra_out, sems.at[2]),
    ]
    copies[0].start()
    copies[1].start()
    slots = spectra.shape[0]
    table = samp[...].T
    for k in range(slots):
        for c in range(2):
            total = None
            for n in range(STEPS):
                row = n * slots + k
                coef = weights[row:row + 1, 0:1]
                first = (n * 2 + c) * nx
                term = coef * table[first:first + nx]
                total = term if total is None else total + term
            spectra[k, c] = total
    copies[2].start()
    for copy in copies:
        copy.wait()


def solution(mesh):
    ngx, ngy = mesh.shape["gx"], mesh.shape["gy"]

    def local(electric, magnetic, material, pml_flags, permittivity, pml_sigma, omega):
        _, nx, ny, nz = electric.shape
        slots = 2 * NFREQ // ngy
        hbm = pl.BlockSpec(memory_space=pltpu.HBM)
        vmem = pl.BlockSpec(memory_space=pltpu.VMEM)
        f32 = jnp.float32
        field = jax.ShapeDtypeStruct(electric.shape, f32)
        e_scratch = pltpu.VMEM((3, nx + 2, ny + 16, nz), f32)
        h_scratch = pltpu.VMEM((3, nx + 1, ny + 8, nz), f32)
        operands = (electric, magnetic, material, pml_flags, permittivity, pml_sigma.reshape(1, nz), omega)
        e_done, h_done, samples, weights = pl.pallas_call(
            functools.partial(kernel, ngx, ngy, nx, ny, nz),
            out_shape=(
                pltpu.VMEM(field.shape, f32),
                pltpu.VMEM(field.shape, f32),
                pltpu.VMEM((ngy * ny, nz), f32),
                pltpu.VMEM((8, nz), f32),
            ),
            in_specs=[hbm] * 7,
            out_specs=(vmem, vmem, vmem, vmem),
            scratch_shapes=[
                e_scratch,
                e_scratch,
                h_scratch,
                h_scratch,
                h_scratch,
                pltpu.VMEM((2, nx, nz), f32),
                pltpu.VMEM((2, nx, nz), f32),
                pltpu.VMEM((6, nx, nz), f32),
                pltpu.VMEM((3, nx, nz), f32),
                pltpu.VMEM((2, nx, nz), f32),
                pltpu.VMEM((2, nx, nz), f32),
                pltpu.VMEM((6, nx + 8, nz), f32),
                pltpu.VMEM((3, nx + 8, nz), f32),
                pltpu.VMEM((2, nx, nz), f32),
                pltpu.VMEM((6, ny, nz), f32),
                pltpu.VMEM((6, ny, nz), f32),
                pltpu.VMEM((nx + 1, ny + 8, nz), jnp.int32),
                pltpu.VMEM((nx, ny, nz), jnp.int32),
                pltpu.VMEM((nx, ny, nz), f32),
                pltpu.VMEM((nx, ny, nz), f32),
                pltpu.SMEM((NMAT,), f32),
                pltpu.VMEM((1, nz), f32),
                pltpu.SMEM((NFREQ,), f32),
                pltpu.SemaphoreType.DMA((8,)),
                pltpu.SemaphoreType.DMA((6,)),
                pltpu.SemaphoreType.DMA((6,)),
                pltpu.SemaphoreType.DMA((6,)),
                pltpu.SemaphoreType.DMA((6,)),
                pltpu.SemaphoreType.DMA((ngy,)),
                pltpu.SemaphoreType.DMA((ngy,)),
            ],
            compiler_params=pltpu.CompilerParams(
                collective_id=0, has_side_effects=True, vmem_limit_bytes=24 * 1024 * 1024),
        )(*[pltpu.with_memory_space_constraint(a, pltpu.HBM) for a in operands])
        spectra = jax.ShapeDtypeStruct((slots, 2, nx, ny * ngy), f32)
        return pl.pallas_call(
            functools.partial(finish, nx),
            out_shape=(field, field, spectra),
            in_specs=[vmem] * 4,
            out_specs=(hbm, hbm, hbm),
            scratch_shapes=[pltpu.VMEM(spectra.shape, f32), pltpu.SemaphoreType.DMA((3,))],
            compiler_params=pltpu.CompilerParams(vmem_limit_bytes=24 * 1024 * 1024),
        )(e_done, h_done, samples, weights)

    placed = (
        P(None, "gx", "gy", None),
        P(None, "gx", "gy", None),
        P("gx", "gy", None),
        P("gx", "gy", None),
        P(),
        P(),
        P(),
    )
    return jax.shard_map(
        local,
        mesh=mesh,
        in_specs=placed,
        out_specs=(P(None, "gx", "gy", None), P(None, "gx", "gy", None), P("gy", None, "gx", None)),
        check_vma=False,
    )
```

```python
import functools

import jax
import jax.numpy as jnp
from jax import lax
from jax.experimental import pallas as pl
from jax.experimental.pallas import tpu as pltpu
from jax.sharding import PartitionSpec as P

STEPS = 2
NFREQ = 8
NMAT = 4
DT = 0.5
MESH = pl.DeviceIdType.MESH

TOP = 8


BLOCK = 4


def blocks(low, high, body, carry=0):
    pairs = (high - low) // (2 * BLOCK)

    def pair(i, carry):
        p = low + i * (2 * BLOCK)
        return body(p + BLOCK, body(p, carry))

    carry = lax.fori_loop(0, pairs, pair, carry)
    for p in range(low + pairs * 2 * BLOCK, high, BLOCK):
        carry = body(p, carry)
    return carry


def kernel(ngx, ngy, nx, ny, nz,
           e_in, h_in, mat_in, flag_in, perm_in, sigma_in, omega_in,
           e_out, h_out, samp, weights,
           e0, e1, h0, h1, h2, down0, down1, up0, up1, above0, above1, below0, below1, rim_h, right0, left0, flag, mat, ek, eg, perm, sigma, omega,
           load_sem, send1, recv1, send2, recv2, send3, recv3):
    gx, gy = lax.axis_index("gx"), lax.axis_index("gy")
    left, right = gx > 0, gx < ngx - 1
    down, up = gy > 0, gy < ngy - 1
    own_x = pl.ds(1, nx)
    own_y = pl.ds(TOP, ny)
    behind, ahead = TOP - 1, TOP + ny
    last = nx + 1

    loads = [
        pltpu.make_async_copy(e_in, e0.at[:, own_x, own_y], load_sem.at[0]),
        pltpu.make_async_copy(h_in, h0.at[:, own_x, own_y], load_sem.at[1]),
        pltpu.make_async_copy(flag_in, flag.at[own_x, own_y], load_sem.at[2]),
        pltpu.make_async_copy(mat_in, mat, load_sem.at[3]),
        pltpu.make_async_copy(sigma_in, sigma, load_sem.at[4]),
        pltpu.make_async_copy(perm_in, perm, load_sem.at[5]),
        pltpu.make_async_copy(omega_in, omega, load_sem.at[6]),
    ]

    barrier = pltpu.get_barrier_semaphore()
    partners = [
        (left, (gx - 1, gy)),
        (right, (gx + 1, gy)),
        (left & up, (gx - 1, gy + 1)),
        (right & down, (gx + 1, gy - 1)),
        (down, (gx, gy - 1)),
        (up, (gx, gy + 1)),
    ]
    if ngy > 4:
        partners += [(jnp.abs(gy - mate) > 3, (gx, mate)) for mate in range(ngy)]
    expected = 0
    for there, device in partners:
        expected = expected + there.astype(jnp.int32)

        @pl.when(there)
        def _():
            pl.semaphore_signal(barrier, inc=1, device_id=device, device_id_type=MESH)

    for copy in loads:
        copy.start()

    @pl.when(jnp.logical_not(right))
    def _():
        for e in (e0, e1):
            for c in (1, 2):
                e[c, last, 0:ahead] = jnp.zeros((ahead, nz), jnp.float32)

    @pl.when(jnp.logical_not(up))
    def _():
        for e, above in ((e0, above0), (e1, above1)):
            e[0, 0, ahead:ahead + 8] = jnp.zeros((8, nz), jnp.float32)
            above[...] = jnp.zeros((2, nx, nz), jnp.float32)

    for e in (e0, e1):
        for c in (0, 2):
            e[c, 1:last, ahead:ahead + 8] = jnp.zeros((nx, 8, nz), jnp.float32)

    def row_of(ref, c, first, r):
        planes, rows = ref.shape[-3], ref.shape[-2]
        return pl.ds((c * planes + first) * rows + r, nx, stride=rows)

    def get_rows(ref, c, first, r):
        return ref.reshape(-1, nz)[row_of(ref, c, first, r), :]

    def put_rows(ref, c, first, r, value):
        ref.reshape(-1, nz)[row_of(ref, c, first, r), :] = value

    def pack_down(e, down_rows):
        for i, c in enumerate((0, 2)):
            down_rows[i] = get_rows(e, c, 1, TOP)

    def pack_up(e, up_rows):
        for c in range(3):
            up_rows[c] = get_rows(e, c, 1, TOP + ny - 1)

    for i in (0, 1, 2):
        loads[i].wait()
    pack_down(e0, down0)
    pack_up(e0, up0)
    for i, c in enumerate((0, 2)):
        up0[3 + i] = get_rows(h0, c, 1, TOP + ny - 1)
    up0[5] = get_rows(flag, 0, 1, TOP + ny - 1).astype(jnp.float32)
    right0[0:3] = e0[:, nx, own_y]
    right0[3:5] = h0[1:3, nx, own_y]
    right0[5] = flag[nx, own_y].astype(jnp.float32)

    pl.semaphore_wait(barrier, expected)

    def remote(src, dst, sends, recvs, i, device):
        return pltpu.make_async_remote_copy(
            src_ref=src, dst_ref=dst, send_sem=sends.at[i], recv_sem=recvs.at[i],
            device_id=device, device_id_type=MESH)

    def e_halo(e, right_planes, behind_planes, down_rows, up_rows, above, below, sends, recvs):
        at = functools.partial(remote, sends=sends, recvs=recvs)
        to_left = [at(e.at[1:3, 1, own_y], e.at[1:3, last, own_y], i=0, device=(gx - 1, gy))]
        to_right = [at(right_planes, behind_planes, i=1, device=(gx + 1, gy))]
        to_down = [at(down_rows, above, i=2, device=(gx, gy - 1))]
        to_up = [at(up_rows, below.at[:, 0:nx], i=3, device=(gx, gy + 1))]
        corner_lu = [at(up_rows.at[1, 0], e.at[1, last, behind], i=4, device=(gx - 1, gy + 1))]
        corner_rd = [at(down_rows.at[0, nx - 1], e.at[0, 0, ahead], i=5, device=(gx + 1, gy - 1))]
        return [
            [left, right, to_left],
            [right, left, to_right],
            [down, up, to_down],
            [up, down, to_up],
            [left & up, right & down, corner_lu],
            [right & down, left & up, corner_rd],
        ]

    def start(plan):
        for sends, _, copies in plan:
            @pl.when(sends)
            def _():
                for copy in copies:
                    copy.start()

    def wait_recv(plan):
        for _, receives, copies in plan:
            @pl.when(receives)
            def _():
                for copy in copies:
                    copy.wait_recv()

    def wait_send(plan):
        for sends, _, copies in plan:
            @pl.when(sends)
            def _():
                for copy in copies:
                    copy.wait_send()

    round1 = e_halo(e0, right0, left0, down0, up0, above0, below0, send1, recv1)
    start(round1[4:6] + round1[0:4])

    loads[4].wait()
    loads[5].wait()
    sg = sigma[...]
    sm = sg * DT / 2.0
    hk1 = (1.0 - sm) / (1.0 + sm)
    hg1 = DT / (1.0 + sm)
    ek1, eg1, eg0 = [], [], []
    for m in range(NMAT):
        eps = jnp.full((1, nz), perm[m], jnp.float32)
        se = sg * DT / (2.0 * eps)
        ek1.append((1.0 - se) / (1.0 + se))
        eg1.append(DT / (eps * (1.0 + se)))
        eg0.append(DT / eps)

    def lanes(f):
        return lax.broadcasted_iota(jnp.int32, f.shape, f.ndim - 1)

    def next_z(f):
        return jnp.where(lanes(f) == nz - 1, 0.0, pltpu.roll(f, nz - 1, f.ndim - 1))

    def prev_z(f):
        return jnp.where(lanes(f) == 0, 0.0, pltpu.roll(f, 1, f.ndim - 1))

    def h_update(e, src, dst, p, planes, r, n, comps, keep=None):
        at, nxt = slice(r, r + n), slice(r + 1, r + n + 1)
        ps, ahead_x = pl.ds(p, planes), pl.ds(p + 1, planes)
        absorbs = flag[ps, at] == 1
        hk = jnp.where(absorbs, hk1, 1.0)
        hg = jnp.where(absorbs, hg1, DT)
        ex, ey, ez = e[0, ps, at], e[1, ps, at], e[2, ps, at]
        curls = (
            lambda: (e[2, ps, nxt] - ez) - (next_z(ey) - ey),
            lambda: (next_z(ex) - ex) - (e[2, ahead_x, at] - ez),
            lambda: (e[1, ahead_x, at] - ey) - (e[0, ps, nxt] - ex),
        )
        for c in comps:
            new = hk * src[c, ps, at] - hg * curls[c]()
            dst[c, ps, at] = new if keep is None else jnp.where(keep, new, 0.0)

    low, high = TOP, TOP + ny
    inner_end = 1 + (nx - 1) // BLOCK * BLOCK

    def h_inner(e, src, dst):
        def body(p, carry):
            h_update(e, src, dst, p, BLOCK, low, ny, (0, 1, 2))
            return carry
        blocks(1, inner_end, body)

    def h_rows(ex, ey, ez, ey_x, ex_y, ez_y, absorbs, hx, hz):
        hk = jnp.where(absorbs, hk1, 1.0)
        hg = jnp.where(absorbs, hg1, DT)
        return (hk * hx - hg * ((ez_y - ez) - (next_z(ey) - ey)),
                hk * hz - hg * ((ey_x - ey) - (ex_y - ex)))

    def h_outer(e, src, dst, down_rows, up_rows, above, below, rim):
        h_update(e, src, dst, 0, 1, low, ny, (1, 2), left)
        h_update(e, src, dst, inner_end, nx + 1 - inner_end, low, ny, (0, 1, 2))
        r = high - 1
        hx, hz = h_rows(
            up_rows[0], up_rows[1], up_rows[2], get_rows(e, 1, 2, r), above[0], above[1],
            get_rows(flag, 0, 1, r) == 1, get_rows(src, 0, 1, r), get_rows(src, 2, 1, r))
        put_rows(dst, 0, 1, r, hx)
        put_rows(dst, 2, 1, r, hz)
        below[1, nx:nx + 1] = e[1, last, behind:behind + 1]
        hx, hz = h_rows(
            below[0, 0:nx], below[1, 0:nx], below[2, 0:nx], below[1, 1:nx + 1], down_rows[0], down_rows[1],
            below0[5, 0:nx] == 1.0, rim[0], rim[1])
        hx, hz = jnp.where(down, hx, 0.0), jnp.where(down, hz, 0.0)
        put_rows(dst, 0, 1, behind, hx)
        put_rows(dst, 2, 1, behind, hz)
        return hx, hz

    def e_update(step, src, h, dst, dst_x, dst_y, comps, p, acc):
        for r in range(0, ny, 8):
            at, below = slice(low + r, low + r + 8), slice(low + r - 1, low + r + 7)
            ps, behind_x = pl.ds(p, BLOCK), pl.ds(p - 1, BLOCK)
            hx, hy, hz = h[0, ps, at], h[1, ps, at], h[2, ps, at]
            keep, gain = ek[behind_x, r:r + 8], eg[behind_x, r:r + 8]
            curls = (
                lambda: (hz - h[2, ps, below]) - (hy - prev_z(hy)),
                lambda: (hx - prev_z(hx)) - (hz - h[2, behind_x, at]),
                lambda: (hy - h[1, behind_x, at]) - (hx - h[0, ps, below]),
            )
            news = {c: keep * src[c, ps, at] + gain * curls[c]() for c in comps}
            for c in comps:
                dst[c, pl.ds(p + dst_x, BLOCK), r + dst_y:r + dst_y + 8] = news[c]
            piece = acc[r // 8]
            for c in (c for c in comps if c < 2):
                for k in range(BLOCK):
                    column = jnp.broadcast_to(news[c][k, :, nz // 2:nz // 2 + 1], (8, nz))
                    piece = jnp.where(lanes(piece) == (step * 2 + c) * nx + p - 1 + k, column, piece)
            acc = acc[:r // 8] + (piece,) + acc[r // 8 + 1:]
        return acc

    loads[3].wait()

    def e_coefficients(p, carry):
        ps = pl.ds(p, BLOCK)
        m = mat[ps]
        absorbs = flag[pl.ds(p + 1, BLOCK), low:high] == 1
        k, g1, g0 = ek1[NMAT - 1], eg1[NMAT - 1], eg0[NMAT - 1]
        for i in range(NMAT - 2, -1, -1):
            here = m == i
            k = jnp.where(here, ek1[i], k)
            g1 = jnp.where(here, eg1[i], g1)
            g0 = jnp.where(here, eg0[i], g0)
        ek[ps] = jnp.where(absorbs, k, 1.0)
        eg[ps] = jnp.where(absorbs, g1, g0)
        return carry

    blocks(0, nx, e_coefficients)
    h_inner(e0, h0, h1)
    wait_recv(round1)
    e0[:, 0, own_y] = left0[0:3]
    h0[1:3, 0, own_y] = left0[3:5]
    flag[0, own_y] = left0[5].astype(jnp.int32)
    rim = h_outer(e0, h0, h1, down0, up0, above0, below0, (below0[3, 0:nx], below0[4, 0:nx]))
    rim_h[0], rim_h[1] = rim
    acc = tuple(jnp.zeros((8, nz), jnp.float32) for _ in range(ny // 8))
    step1 = functools.partial(e_update, 0, e0, h1, e1, 0, TOP, (0, 1, 2))
    round2 = e_halo(e1, e1.at[:, nx, own_y], e1.at[:, 0, own_y], down1, up1, above1, below1, send2, recv2)

    def e_rows(y, comps, out):
        r = TOP + y
        hx, hy, hz = (get_rows(h1, c, 1, r) for c in range(3))
        keep, gain = get_rows(ek, 0, 0, y), get_rows(eg, 0, 0, y)
        curls = (
            lambda: (hz - get_rows(h1, 2, 1, r - 1)) - (hy - prev_z(hy)),
            lambda: (hx - prev_z(hx)) - (hz - get_rows(h1, 2, 0, r)),
            lambda: (hy - get_rows(h1, 1, 0, r)) - (hx - get_rows(h1, 0, 1, r - 1)),
        )
        for i, c in enumerate(comps):
            out[i] = keep * get_rows(e0, c, 1, r) + gain * curls[c]()

    acc = step1(1, acc)
    acc = step1(nx + 1 - BLOCK, acc)
    start(round2[0:2])
    e_rows(ny - 1, (0, 1, 2), up1)
    e_rows(0, (0, 2), down1)
    start(round2[4:6] + round2[2:4])
    acc = blocks(1 + BLOCK, nx + 1 - BLOCK, step1, acc)

    h_inner(e1, h1, h2)
    wait_recv(round2)
    h_outer(e1, h1, h2, down1, up1, above1, below1, (rim_h[0], rim_h[1]))
    step2 = functools.partial(e_update, 1, e1, h2, e_out, -1, 0)
    acc = blocks(1, nx + 1, functools.partial(step2, (0, 1)), acc)
    mine = pl.ds(pl.multiple_of(gy * ny, ny), ny)
    samp[mine] = jnp.concatenate(acc, axis=0)
    round3 = []
    for d in range(1, ngy):
        mate = lax.rem(gy + d, ngy)
        copy = pltpu.make_async_remote_copy(
            src_ref=samp.at[mine], dst_ref=samp.at[mine], send_sem=send3.at[d], recv_sem=recv3.at[d],
            device_id=(gx, mate), device_id_type=MESH)
        copy.start()
        round3.append(copy)
    blocks(1, nx + 1, functools.partial(step2, (2,)), acc)
    h_out[...] = h2[:, 1:nx + 1, low:high]
    loads[6].wait()
    slots = 2 * NFREQ // ngy
    rows = lax.broadcasted_iota(jnp.int32, (8, nz), 0)
    angle = jnp.zeros((8, nz), jnp.float32)
    is_cos = jnp.zeros((8, nz), jnp.bool_)
    for n in range(STEPS):
        for k in range(slots):
            here = rows == n * slots + k
            slot = gy * slots + k
            angle = jnp.where(here, omega[lax.rem(slot, NFREQ)] * ((n + 1) * DT), angle)
            is_cos = is_cos | (here & (slot < NFREQ))
    weights[...] = jnp.where(is_cos, jnp.cos(angle), -jnp.sin(angle))
    wait_send(round1)
    wait_send(round2)
    for copy in round3:
        copy.wait_recv()
    for copy in round3:
        copy.wait_send()


def finish(nx, e_in, h_in, samp, weights, e_out, h_out, spectra_out, spectra, sems):
    copies = [
        pltpu.make_async_copy(e_in, e_out, sems.at[0]),
        pltpu.make_async_copy(h_in, h_out, sems.at[1]),
        pltpu.make_async_copy(spectra, spectra_out, sems.at[2]),
    ]
    copies[0].start()
    copies[1].start()
    slots = spectra.shape[0]
    table = samp[...].T
    for k in range(slots):
        for c in range(2):
            total = None
            for n in range(STEPS):
                row = n * slots + k
                coef = weights[row:row + 1, 0:1]
                first = (n * 2 + c) * nx
                term = coef * table[first:first + nx]
                total = term if total is None else total + term
            spectra[k, c] = total
    copies[2].start()
    for copy in copies:
        copy.wait()


def solution(mesh):
    ngx, ngy = mesh.shape["gx"], mesh.shape["gy"]

    def local(electric, magnetic, material, pml_flags, permittivity, pml_sigma, omega):
        _, nx, ny, nz = electric.shape
        slots = 2 * NFREQ // ngy
        hbm = pl.BlockSpec(memory_space=pltpu.HBM)
        vmem = pl.BlockSpec(memory_space=pltpu.VMEM)
        f32 = jnp.float32
        field = jax.ShapeDtypeStruct(electric.shape, f32)
        e_scratch = pltpu.VMEM((3, nx + 2, ny + 16, nz), f32)
        h_scratch = pltpu.VMEM((3, nx + 1, ny + 8, nz), f32)
        operands = (electric, magnetic, material, pml_flags, permittivity, pml_sigma.reshape(1, nz), omega)
        e_done, h_done, samples, weights = pl.pallas_call(
            functools.partial(kernel, ngx, ngy, nx, ny, nz),
            out_shape=(
                pltpu.VMEM(field.shape, f32),
                pltpu.VMEM(field.shape, f32),
                pltpu.VMEM((ngy * ny, nz), f32),
                pltpu.VMEM((8, nz), f32),
            ),
            in_specs=[hbm] * 7,
            out_specs=(vmem, vmem, vmem, vmem),
            scratch_shapes=[
                e_scratch,
                e_scratch,
                h_scratch,
                h_scratch,
                h_scratch,
                pltpu.VMEM((2, nx, nz), f32),
                pltpu.VMEM((2, nx, nz), f32),
                pltpu.VMEM((6, nx, nz), f32),
                pltpu.VMEM((3, nx, nz), f32),
                pltpu.VMEM((2, nx, nz), f32),
                pltpu.VMEM((2, nx, nz), f32),
                pltpu.VMEM((6, nx + 8, nz), f32),
                pltpu.VMEM((3, nx + 8, nz), f32),
                pltpu.VMEM((2, nx, nz), f32),
                pltpu.VMEM((6, ny, nz), f32),
                pltpu.VMEM((6, ny, nz), f32),
                pltpu.VMEM((nx + 1, ny + 8, nz), jnp.int32),
                pltpu.VMEM((nx, ny, nz), jnp.int32),
                pltpu.VMEM((nx, ny, nz), f32),
                pltpu.VMEM((nx, ny, nz), f32),
                pltpu.SMEM((NMAT,), f32),
                pltpu.VMEM((1, nz), f32),
                pltpu.SMEM((NFREQ,), f32),
                pltpu.SemaphoreType.DMA((7,)),
                pltpu.SemaphoreType.DMA((6,)),
                pltpu.SemaphoreType.DMA((6,)),
                pltpu.SemaphoreType.DMA((6,)),
                pltpu.SemaphoreType.DMA((6,)),
                pltpu.SemaphoreType.DMA((ngy,)),
                pltpu.SemaphoreType.DMA((ngy,)),
            ],
            compiler_params=pltpu.CompilerParams(
                collective_id=0, has_side_effects=True, vmem_limit_bytes=24 * 1024 * 1024),
        )(*[pltpu.with_memory_space_constraint(a, pltpu.HBM) for a in operands])
        spectra = jax.ShapeDtypeStruct((slots, 2, nx, ny * ngy), f32)
        return pl.pallas_call(
            functools.partial(finish, nx),
            out_shape=(field, field, spectra),
            in_specs=[vmem] * 4,
            out_specs=(hbm, hbm, hbm),
            scratch_shapes=[pltpu.VMEM(spectra.shape, f32), pltpu.SemaphoreType.DMA((3,))],
            compiler_params=pltpu.CompilerParams(vmem_limit_bytes=24 * 1024 * 1024),
        )(e_done, h_done, samples, weights)

    placed = (
        P(None, "gx", "gy", None),
        P(None, "gx", "gy", None),
        P("gx", "gy", None),
        P("gx", "gy", None),
        P(),
        P(),
        P(),
    )
    return jax.shard_map(
        local,
        mesh=mesh,
        in_specs=placed,
        out_specs=(P(None, "gx", "gy", None), P(None, "gx", "gy", None), P("gy", None, "gx", None)),
        check_vma=False,
    )
```
